256 devices in a mesh: seq: 32 (over z, x), head: 8 (over y, core).
Axes of the slice: x: 4, y: 4, z: 8, core: 2. Of those that a mesh axis runs over, the one named last changes fastest.
Arguments:
- states: bfloat16 [16384, 4096], P('seq'), may hold values from -6 to 256
- w_query: bfloat16 [4096, 4096], P('seq', 'head'), may hold values from -1 to 1
- w_output: bfloat16 [4096, 4096], P('head', 'seq'), may hold values from -0.09375 to 0.09375
- kv_store: bfloat16 [256, 2, 128, 4096], P('seq', None, None, 'head'), may hold values from -140 to 140
- neighbour_ids: int32 [256, 2], P('seq'), may hold values from 0 to 255, as said below
- block_row: int32 [256], replicated, may hold values from 0 to 255, as said below
Outputs:
- mixed: bfloat16 [16384, 4096], P('seq', 'head')
The draws below stay inside these ranges and needn't reach their ends.
Inputs may be any that keep to these rules, and one draw needn't show every extreme that they name: `block_row`: A permutation of 0 to 255; row r of kv_store lies on index r // 8 of seq. `neighbour_ids`: of the 16 neighbours of one index of seq, at most 2 lie in rows of kv_store held by any one index of seq; one such holder has exactly 2 of every index's neighbours.
All inputs are finite; a program needn't handle non-finite values.
Results may differ from the reference program's by a relative error of at most 0.019.
Values may be sent and summed in bfloat16 or wider, within the bound.
A program may use at most 128 MiB of HBM per device.

```python
import jax
import jax.numpy as jnp
from jax import lax

D = 4096
HD = 128
STRETCH = 64
NB_TOK = 128
NEIGH = 2
TOK_DEV = 512
BLK_DEV = 8
SEQ = 16384
HH = 4096
TOKENS = 16384
STRETCHES = 256
BLOCKS = 256
SLOTS = 2
N_SEQ = 32
N_HEAD = 8


def shared_pattern(key):
    column = jax.random.randint(jax.random.fold_in(key, 31), (), 0, D).astype(jnp.int32)
    sign_row = jnp.where(jax.random.bernoulli(jax.random.fold_in(key, 32), 0.5, (HH,)), 1.0, -1.0).astype(jnp.float32)
    return (column, sign_row)


def ordering(key):
    return jax.random.permutation(jax.random.fold_in(key, 7), BLOCKS).astype(jnp.int32)


def draw_block_row(key, part):
    return ordering(key)


def draw_neighbour_ids(key, part):
    order = ordering(key)
    inverse = jnp.argsort(order).astype(jnp.int32)
    requests = TOK_DEV // STRETCH * NEIGH
    hottest = jax.random.randint(jax.random.fold_in(key, 8), (), 0, N_SEQ).astype(jnp.int32)
    device_keys = jax.random.split(jax.random.fold_in(key, 9), N_SEQ)

    def one_device(dev_key):
        key_a, key_b, key_c = jax.random.split(dev_key, 3)
        others = jax.random.permutation(key_a, N_SEQ - 1).astype(jnp.int32)
        others = others + (others >= hottest).astype(jnp.int32)
        position = jnp.arange(requests, dtype=jnp.int32)
        picks = others[jnp.maximum(position - SLOTS, 0) % (N_SEQ - 1)]
        holders = jnp.where(position < SLOTS, hottest, picks)
        within = jax.random.randint(key_b, (requests,), 0, BLK_DEV).astype(jnp.int32)
        shuffled = jax.random.permutation(key_c, holders * BLK_DEV + within)
        return inverse[shuffled]
    return jax.vmap(one_device)(device_keys).reshape(STRETCHES, NEIGH).astype(jnp.int32)


def draw_states(key, part):
    key = jax.random.fold_in(key, 13)
    result = jnp.clip(jax.random.normal(key, (TOKENS, D), jnp.float32), -6.0, 6.0)
    return result.astype(jnp.bfloat16)


def draw_w_query(key, part):
    column, sign_row = shared_pattern(key)
    key = jax.random.fold_in(key, 14)
    row_scale = D ** (-0.5)
    base_draw = jnp.clip(jax.random.normal(key, (D, HH), jnp.float32), -6.0, 6.0) * row_scale
    chosen_row = jnp.arange(D, dtype=jnp.int32) == column
    return jnp.where(chosen_row[:, None], sign_row[None, :] * row_scale, base_draw).astype(jnp.bfloat16)


def draw_kv_store(key, part):
    key = jax.random.fold_in(key, 5)
    key_a, key_b = jax.random.split(key, 2)
    key_rows = jnp.clip(jax.random.normal(key_a, (BLOCKS, NB_TOK, HH), jnp.float32), -6.0, 6.0)
    value_rows = 3.0 * jnp.clip(jax.random.normal(key_b, (BLOCKS, NB_TOK, HH), jnp.float32), -6.0, 6.0)
    return jnp.stack([key_rows, value_rows], axis=1).astype(jnp.bfloat16)


def steps_of(rng, shape, cuts, smallest, top_value):
    gain, own = 1.0, jax.random.fold_in(rng, 6)
    for dim, blocks in cuts:
        heights = jnp.exp(jax.random.uniform(jax.random.fold_in(own, dim), (blocks,), jnp.float32, smallest / len(cuts), top_value / len(cuts)))
        gain = gain * jnp.repeat(heights, shape[dim] // blocks).reshape([-1 if axis == dim else 1 for axis in range(len(shape))])
    return gain


def normal_values(own_key, extent, scale, bound, shards=(), kind=jnp.bfloat16):
    level = steps_of(own_key, extent, shards, -0.22, 0.18) if shards else 1.0
    array = jax.random.normal(own_key, extent, jnp.float32) * scale * level
    return jnp.minimum(jnp.maximum(array, -bound), bound).astype(kind)


def setup_inputs(seed: int = 0) -> dict:
    key_list = jax.random.split(jax.random.key(seed), 7)
    return {
        "states": draw_states(jax.random.fold_in(key_list[6], 71), 0),
        "w_query": draw_w_query(jax.random.fold_in(key_list[6], 71), 0),
        "w_output": normal_values(key_list[2], (HH, D), HH ** -0.5, 0.09375, ((0, 8), (1, 32))),
        "kv_store": draw_kv_store(jax.random.fold_in(key_list[6], 71), 0),
        "neighbour_ids": draw_neighbour_ids(jax.random.fold_in(key_list[6], 71), 0),
        "block_row": draw_block_row(jax.random.fold_in(key_list[6], 71), 0),
    }


def partial_attend(query_block, kv_blocks):
    count, rows, width = query_block.shape
    nheads = width // HD
    qhead = query_block.reshape(count, rows, nheads, HD).astype(jnp.float32)
    keys = kv_blocks[:, 0].reshape(count, NB_TOK, nheads, HD).astype(jnp.float32)
    values = kv_blocks[:, 1].reshape(count, NB_TOK, nheads, HD).astype(jnp.float32)
    scores = jnp.einsum("nqhd,nkhd->nhqk", qhead, keys) * (1.0 / (HD ** 0.5))
    maxima = jnp.max(scores, axis=-1)
    weights = jnp.exp(scores - maxima[..., None]).astype(jnp.bfloat16)
    weights = lax.optimization_barrier(weights).astype(jnp.float32)
    totals = jnp.sum(weights, axis=-1)
    outputs = jnp.einsum("nhqk,nkhd->nqhd", weights, values).reshape(count, rows, width)
    return outputs, maxima, totals


def combine_pair(outputs, maxima, totals):
    spans, neigh, rows, width = outputs.shape
    nheads = width // HD
    top = jnp.max(maxima, axis=1)
    factor = jnp.exp(maxima - top[:, None])
    denom = jnp.sum(factor * totals, axis=1)
    spread = jnp.transpose(factor, (0, 1, 3, 2))[..., None]
    numer = jnp.sum(outputs.reshape(spans, neigh, rows, nheads, HD) * spread, axis=1)
    result = numer / jnp.transpose(denom, (0, 2, 1))[..., None]
    return result.reshape(spans, rows, width).astype(jnp.bfloat16)


def reference(states, w_query, w_output, kv_store, neighbour_ids, block_row):
    queries = jnp.dot(states, w_query, preferred_element_type=jnp.float32).astype(jnp.bfloat16)
    seq_count = TOKENS // SEQ
    padding = jnp.zeros((seq_count, STRETCH - 1, HH), jnp.bfloat16)
    per_seq = queries.reshape(seq_count, SEQ, HH)
    groups = jnp.concatenate([per_seq[:, STRETCH - 1:], padding], axis=1).reshape(STRETCHES, STRETCH, HH)

    def one_stretch(pair):
        group, chosen = pair
        blocks = kv_store[block_row[chosen]]
        repeated = jnp.broadcast_to(group[None], (NEIGH, STRETCH, HH))
        outputs, maxima, totals = partial_attend(repeated, blocks)
        return combine_pair(outputs[None], maxima[None], totals[None])[0]

    context_groups = lax.map(one_stretch, (groups, neighbour_ids))
    flat = context_groups.reshape(seq_count, SEQ, HH)
    context = jnp.concatenate([padding, flat[:, :SEQ - STRETCH + 1]], axis=1).reshape(TOKENS, HH)
    span = HH // N_HEAD
    mixed = jnp.zeros((TOKENS, D), jnp.float32)
    for group in range(N_HEAD):
        part_sum = jnp.dot(context[:, group * span:(group + 1) * span], w_output[group * span:(group + 1) * span], preferred_element_type=jnp.float32).astype(jnp.bfloat16)
        mixed = mixed + lax.optimization_barrier(part_sum).astype(jnp.float32)
    return mixed.astype(jnp.bfloat16)
```

```python
import jax
import jax.numpy as jnp
from jax import lax
from jax.experimental import pallas as pl
from jax.experimental.pallas import tpu as pltpu
from jax.sharding import PartitionSpec as P

HD = 128
STRETCH = 64
NB_TOK = 128
NX, NZ, NY = 4, 8, 4
NSEQ, NHEAD = NX * NZ, 2 * NY
T = 512
W = 512
QT = 128
NEG = -1e30
SCALE = 1.0 / HD**0.5
MESH = pl.DeviceIdType.MESH
N_COPIES = 192
BF = jnp.bfloat16
F32 = jnp.float32


def quarter(i):
    return pl.ds(i * QT, QT)


def part(i):
    return pl.ds(pl.multiple_of(i * QT, QT), QT)


def kernel(
    states, wq, wo, kv, rows, out,
    st, wqg, acc, qall, kvr, oatt, ml, ro, sw, rw, wog, rall, rsm,
    ctx, ps, pr, tf, t2s, t2r, t1s, t1r, ost, lsem, osem, ssem, rsem,
):
    s, h = lax.axis_index("seq"), lax.axis_index("head")
    z, x, y, c = s // NX, s % NX, h // 2, h % 2
    up, down = (s + NX) % NSEQ, (s + NSEQ - NX) % NSEQ
    right, left = z * NX + (x + 1) % NX, z * NX + (x + NX - 1) % NX
    after, before = (s + 1) % NSEQ, (s + NSEQ - 1) % NSEQ
    yup, ydown, twin = (h + 2) % NHEAD, (h + NHEAD - 2) % NHEAD, h + 1 - 2 * c
    count = [0]
    started = {}

    def send(src, dst, seq=None, head=None):
        n = count[0]
        count[0] += 1
        copy = pltpu.make_async_remote_copy(
            src_ref=src,
            dst_ref=dst,
            send_sem=ssem.at[n],
            recv_sem=rsem.at[n],
            device_id=(s if seq is None else seq, h if head is None else head),
            device_id_type=MESH,
        )
        copy.start()
        started[id(copy)] = copy
        return copy

    barrier = pltpu.get_barrier_semaphore()
    peers = [((s + NX * i) % NSEQ, h) for i in range(1, NZ)]
    peers += [(right, h), (left, h), (after, h), (before, h)]
    peers += [(s, (h + i) % NHEAD) for i in range(1, NHEAD)]
    for peer in peers:
        pl.semaphore_signal(barrier, inc=1, device_id=peer, device_id_type=MESH)

    own = [
        pltpu.make_async_copy(states, st.at[pl.ds(0, T)], lsem.at[0]),
        pltpu.make_async_copy(wq, wqg.at[0, part(x)], lsem.at[1]),
        pltpu.make_async_copy(wo, wog.at[z, x], lsem.at[2]),
        pltpu.make_async_copy(kv, kvr.at[pl.ds(x * 8, 8)], lsem.at[3]),
        pltpu.make_async_copy(rows, rall.at[0], lsem.at[4]),
    ]
    for copy in own:
        copy.start()
    pl.semaphore_wait(barrier, len(peers))

    wx = {}
    wx[1] = send(wq, wqg.at[0, part(x)], seq=right)
    wx[3] = send(wq, wqg.at[0, part(x)], seq=left)
    wup, wdown = {}, {}

    def wsend(j, d, first=False):
        at = part((x + NX - d) % NX)
        src = wq if first else wqg.at[j, at]
        if j < 3 or (j == 3 and d in (0, 1)):
            wup[j + 1, d] = send(src, wqg.at[j + 1, at], seq=up)
        if j in (0, 7, 6) or (j == 5 and d in (2, 3)):
            wdown[(j + 7) % 8, d] = send(src, wqg.at[(j + 7) % 8, at], seq=down)

    wsend(0, 0, first=True)
    oup, odown = {}, {}

    def osend(step):
        if step == 1:
            oup[1] = send(wo, wog.at[z, x], seq=up)
            odown[1] = send(wo, wog.at[z, x], seq=down)
            return
        oup[step - 1].wait_recv()
        a = (z + NZ - step + 1) % NZ
        if step < 4:
            oup[step] = send(wog.at[a, x], wog.at[a, x], seq=up)
        else:
            half = pl.ds(0, 256)
            oup[step] = send(wog.at[a, x, half], wog.at[a, x, half], seq=up)
        odown[step - 1].wait_recv()
        b = (z + step - 1) % NZ
        if step < 4:
            odown[step] = send(wog.at[b, x], wog.at[b, x], seq=down)
        else:
            half = pl.ds(256, 256)
            odown[step] = send(wog.at[b, x, half], wog.at[b, x, half], seq=down)

    osend(1)
    rids = [
        send(rows, rall.at[i], seq=(s + NX * i) % NSEQ) for i in range(1, NZ)
    ]
    hcols = pl.ds(pl.multiple_of(h * W, W), W)
    tail = st.at[pl.ds(T, 64), hcols]
    first_rows = send(states.at[pl.ds(0, 64), hcols], tail, seq=before)

    own[1].wait()
    wx[1].wait_recv()
    lo, hi = (x + 3) % NX, (x + 1) % NX
    halves = [
        wqg.at[0, pl.ds(pl.multiple_of(lo * QT, QT), 64)],
        wqg.at[0, pl.ds(pl.multiple_of(hi * QT + 64, 64), 64)],
    ]
    wx[2] = send(halves[0], halves[0], seq=right)
    wsend(0, 1)
    wx[3].wait_recv()
    wx[4] = send(halves[1], halves[1], seq=left)
    wsend(0, 3)

    def blocks(xo, half):
        return kvr.at[pl.ds(xo * 8 + 4 * half, 4)]

    kvs = {}
    kvs["r0"] = send(kv.at[pl.ds(0, 4)], blocks(x, 0), seq=right)
    kvs["l1"] = send(kv.at[pl.ds(4, 4)], blocks(x, 1), seq=left)
    kvs["r1"] = send(kv.at[pl.ds(4, 4)], blocks(x, 1), seq=right)
    kvs["l0"] = send(kv.at[pl.ds(0, 4)], blocks(x, 0), seq=left)

    wx[2].wait_recv()
    wx[4].wait_recv()
    wsend(0, 2)

    first_rows.wait_recv()
    others = [send(tail, tail, head=(h + i) % NHEAD) for i in range(1, NHEAD)]
    osend(2)

    def multiply(j):
        cols = pl.ds(pl.multiple_of(((z + NZ - j) % NZ) * 512, 512), 512)

        def body(i, _):
            r = pl.ds(pl.multiple_of(i * 192, 64), 192)
            term = jnp.dot(st[r, cols], wqg[j], preferred_element_type=F32)
            acc[r, :] = term if j == 0 else acc[r, :] + term
            return 0

        lax.fori_loop(0, 3, body, 0)

    order = (0, 1, 3, 2)
    for j in (1, 2, 3):
        for d in order:
            wup[j, d].wait_recv()
            wdown[8 - j, d].wait_recv()
            wsend(j, d)
            wsend(8 - j, d)
        if j == 1:
            own[0].wait()
            for copy in others:
                copy.wait_recv()
            for copy in others:
                copy.wait_send()
                del started[id(copy)]

            @pl.when(s == NSEQ - 1)
            def _():
                st[pl.ds(T, 64), :] = jnp.zeros((64, NHEAD * W), BF)

            multiply(0)
        if j == 3:
            kvs["r0"].wait_recv()
            kvs["r2"] = send(blocks(lo, 0), blocks(lo, 0), seq=right)
            kvs["l1"].wait_recv()
            kvs["l2"] = send(blocks(hi, 1), blocks(hi, 1), seq=left)
        if j < 3:
            osend(j + 2)
        multiply(j)
        multiply(8 - j)
    for d in (0, 1):
        wup[4, d].wait_recv()
    for d in (2, 3):
        wdown[4, d].wait_recv()
    multiply(4)

    qup, qdown = {}, {}

    def qsend(j, q):
        at = qall.at[j, quarter(q)]
        if j < 3 or (j == 3 and q < 2):
            qup[j + 1, q] = send(at, qall.at[j + 1, quarter(q)], seq=up)
        if j in (0, 7, 6) or (j == 5 and q >= 2):
            k = (j + 7) % 8
            qdown[k, q] = send(at, qall.at[k, quarter(q)], seq=down)

    for q in range(4):
        qall[0, quarter(q), :] = acc[pl.ds(63 + q * QT, QT), :].astype(BF)
        qsend(0, q)

    for copy in rids:
        copy.wait_recv()
    own[4].wait()
    scalars = pltpu.make_async_copy(rall, rsm, lsem.at[5])
    scalars.start()
    oup[4].wait_recv()
    odown[4].wait_recv()
    scalars.wait()

    for j in (1, 2):
        for q in range(4):
            qup[j, q].wait_recv()
            qdown[8 - j, q].wait_recv()
            qsend(j, q)
            qsend(8 - j, q)

    own[3].wait()
    for name in ("r1", "l0", "r2", "l2"):
        kvs[name].wait_recv()

    own[2].wait()
    oxs = {}
    oxs["r"] = send(wog.at[:, x], wog.at[:, x], seq=right)
    oxs["l"] = send(wog.at[:, x], wog.at[:, x], seq=left)

    lane = lax.broadcasted_iota(jnp.int32, (STRETCH, 128), 1)
    wide = lax.broadcasted_iota(jnp.int32, (1, 2 * NB_TOK), 1)

    def attend(j, g):
        r0, r1 = rsm[j, g, 0], rsm[j, g, 1]
        off0 = jnp.where(r0 // 32 == z, 0.0, NEG)
        off1 = jnp.where(r1 // 32 == z, 0.0, NEG)
        bias = jnp.where(wide < NB_TOK, off0, off1)
        b0, b1 = r0 % 32, r1 % 32
        at = pl.ds(pl.multiple_of(g * STRETCH, STRETCH), STRETCH)
        stats = jnp.zeros((STRETCH, 128), F32)
        for i in range(W // HD):
            cols = slice(i * HD, i * HD + HD)
            keys = jnp.concatenate([kvr[b0, 0, :, cols], kvr[b1, 0, :, cols]], axis=0)
            scores = lax.dot_general(
                qall[j, at, cols], keys, (((1,), (1,)), ((), ())), preferred_element_type=F32
            )
            scores = scores * SCALE + bias
            top = jnp.max(scores, axis=1, keepdims=True)
            weights = jnp.exp(scores - top).astype(BF)
            total = jnp.sum(weights.astype(F32), axis=1, keepdims=True)
            values = jnp.concatenate([kvr[b0, 1, :, cols], kvr[b1, 1, :, cols]], axis=0)
            got = jnp.dot(weights, values, preferred_element_type=F32)
            oatt[j, at, cols] = got.astype(BF)
            stats = jnp.where(lane == i, top, jnp.where(lane == i + 4, total, stats))
        ml[j, at, :] = stats

    def attend_slots(a, b):
        def body(i, _):
            attend(jnp.where(i < 8, a, b), i % 8)
            return 0

        lax.fori_loop(0, 8 if a == b else 16, body, 0)

    attend_slots(1, 7)
    for q in range(4):
        if q < 2:
            qup[3, q].wait_recv()
            qsend(3, q)
        else:
            qdown[5, q].wait_recv()
            qsend(5, q)
    attend_slots(2, 6)
    for q in range(4):
        if q < 2:
            qdown[5, q].wait_recv()
        else:
            qup[3, q].wait_recv()
    attend_slots(3, 5)
    for q in range(4):
        (qup if q < 2 else qdown)[4, q].wait_recv()
    attend_slots(4, 4)

    sent, sent_stats = {}, {}

    def rsend(way, k, q, rows_at):
        j = k if way == 0 else 8 - k
        there = down if way == 0 else up
        sent[way, k, q] = send(oatt.at[j, rows_at], ro.at[way, k - 1, rows_at], seq=there)
        sent_stats[way, k, q] = send(sw.at[j, q], rw.at[way, k - 1, q], seq=there)

    def turn_out(j, q):
        sw[j, q] = jnp.transpose(ml[j, quarter(q), :])[0:8, :]

    def turn_in(way, k, q):
        wire = jnp.concatenate([rw[way, k - 1, q], jnp.zeros((120, 128), F32)], axis=0)
        return jnp.transpose(wire)

    def merge(way, k, q, start, size):
        j = k if way == 0 else 8 - k
        at = pl.ds(q * QT + start, size)
        a = turn_in(way, k + 1, q)[start : start + size]
        b = ml[j, at, :]
        top = jnp.maximum(a, b)
        ea, eb = jnp.exp(a - top), jnp.exp(b - top)
        total = a * pltpu.roll(ea, 4, axis=1) + b * pltpu.roll(eb, 4, axis=1)
        lanes = lax.broadcasted_iota(jnp.int32, (size, 128), 1)
        ml[j, at, :] = jnp.where(lanes < 4, top, jnp.where(lanes < 8, total, 0.0))
        for i in range(W // HD):
            cols = slice(i * HD, i * HD + HD)
            mixed = ea[:, i : i + 1] * ro[way, k, at, cols].astype(F32)
            mixed = mixed + eb[:, i : i + 1] * oatt[j, at, cols].astype(F32)
            oatt[j, at, cols] = mixed.astype(BF)

    for q in range(4):
        turn_out(4, q)
        rsend(0, 4, q, pl.ds(q * QT, 64))
        rsend(1, 4, q, pl.ds(q * QT + 64, 64))
    for k in (3, 2, 1):
        if k == 2:
            attend_slots(0, 0)
            oxs["r"].wait_recv()
            lower = wog.at[pl.ds(0, 4), lo]
            oxs["r2"] = send(lower, lower, seq=right)
            oxs["l"].wait_recv()
            upper = wog.at[pl.ds(4, 4), hi]
            oxs["l2"] = send(upper, upper, seq=left)
        for q in range(4):
            for way in (0, 1):
                sent[way, k + 1, q].wait_recv()
                sent_stats[way, k + 1, q].wait_recv()
                if k == 3:
                    merge(way, k, q, 64 * way, 64)
                else:
                    merge(way, k, q, 0, QT)
                turn_out(k if way == 0 else 8 - k, q)
                rsend(way, k, q, quarter(q))
    for name in ("r2", "l2"):
        oxs[name].wait_recv()

    def weights_for(g):
        return jnp.concatenate([wog[g, i] for i in range(NX)], axis=1)

    def join(q):
        at = quarter(q)
        for way in (0, 1):
            sent[way, 1, q].wait_recv()
            sent_stats[way, 1, q].wait_recv()
        a, b, e = turn_in(0, 1, q), turn_in(1, 1, q), ml[0, at, :]
        top = jnp.maximum(jnp.maximum(a, b), e)
        fa, fb, fe = jnp.exp(a - top), jnp.exp(b - top), jnp.exp(e - top)
        total = a * pltpu.roll(fa, 4, axis=1) + b * pltpu.roll(fb, 4, axis=1)
        total = total + e * pltpu.roll(fe, 4, axis=1)
        total = pltpu.roll(total, 124, axis=1)
        fa, fb, fe = fa / total, fb / total, fe / total
        for i in range(W // HD):
            cols = slice(i * HD, i * HD + HD)
            mixed = fa[:, i : i + 1] * ro[0, 0, at, cols].astype(F32)
            mixed = mixed + fb[:, i : i + 1] * ro[1, 0, at, cols].astype(F32)
            mixed = mixed + fe[:, i : i + 1] * oatt[0, at, cols].astype(F32)
            ctx[q, :, cols] = mixed.astype(BF)

    pairs, seconds, thirds, written = {}, {}, {}, []

    def for_twin(q):
        def body(i, _):
            g = 2 * ((y + i) % NY) + 1 - c
            ps[q, i] = jnp.dot(ctx[q], weights_for(g), preferred_element_type=F32).astype(BF)
            return 0

        lax.fori_loop(0, NY, body, 0)
        pairs[q] = send(ps.at[q], pr.at[q], head=twin)

    def for_self(q):
        pairs[q].wait_recv()

        def body(i, _):
            g = 2 * ((y + i) % NY) + c
            term = jnp.dot(ctx[q], weights_for(g), preferred_element_type=F32)
            tf[q, i] = term + pr[q, i].astype(F32)
            return 0

        lax.fori_loop(0, NY, body, 0)
        t2s[q] = tf[q, 2].astype(BF)
        a, b = pl.ds(0, 64), pl.ds(64, 64)
        seconds[q] = (
            send(t2s.at[q, a], t2r.at[q, a], head=yup),
            send(t2s.at[q, b], t2r.at[q, b], head=ydown),
        )

    def pass_on(q):
        for copy in seconds[q]:
            copy.wait_recv()
        t1s[q, 0, 0:64] = (tf[q, 1, 0:64] + t2r[q, 0:64].astype(F32)).astype(BF)
        t1s[q, 0, 64:128] = tf[q, 1, 64:128].astype(BF)
        t1s[q, 1, 0:64] = tf[q, 3, 0:64].astype(BF)
        t1s[q, 1, 64:128] = (tf[q, 3, 64:128] + t2r[q, 64:128].astype(F32)).astype(BF)
        thirds[q] = (
            send(t1s.at[q, 0], t1r.at[q, 0], head=yup),
            send(t1s.at[q, 1], t1r.at[q, 1], head=ydown),
        )

    def finish(q):
        for copy in thirds[q]:
            copy.wait_recv()
        total = tf[q, 0] + t1r[q, 0].astype(F32) + t1r[q, 1].astype(F32)
        ost[q] = total.astype(BF)
        copy = pltpu.make_async_copy(ost.at[q], out.at[quarter(q)], osem.at[q])
        copy.start()
        written.append(copy)

    for step in range(7):
        for q in range(4):
            if step == q:
                join(q)
                for_twin(q)
        for lag, act in ((1, for_self), (2, pass_on), (3, finish)):
            if 0 <= step - lag < 4:
                act(step - lag)
    for copy in written:
        copy.wait()
    for copy in started.values():
        copy.wait_send()


def exchange(states, w_query, w_output, kv_store, rows):
    anywhere = pl.BlockSpec(memory_space=pl.ANY)
    vm = pltpu.VMEM
    return pl.pallas_call(
        kernel,
        out_shape=jax.ShapeDtypeStruct((T, W), BF),
        in_specs=[anywhere] * 4 + [pl.BlockSpec(memory_space=vm)],
        out_specs=anywhere,
        scratch_shapes=[
            vm((T + 64, NHEAD * W), BF),
            vm((NZ, 512, W), BF),
            vm((T + 64, W), F32),
            vm((NZ, T, W), BF),
            vm((32, 2, NB_TOK, W), BF),
            vm((NZ, T, W), BF),
            vm((NZ, T, 128), F32),
            vm((2, 4, T, W), BF),
            vm((NZ, 4, 8, 128), F32),
            vm((2, 4, 4, 8, 128), F32),
            vm((NZ, NX, W, 128), BF),
            vm((NZ, 8, 128), jnp.int32),
            pltpu.SMEM((NZ, 8, 128), jnp.int32),
            vm((4, QT, W), BF),
            vm((4, NY, QT, 512), BF),
            vm((4, NY, QT, 512), BF),
            vm((4, NY, QT, 512), F32),
            vm((4, QT, 512), BF),
            vm((4, QT, 512), BF),
            vm((4, 2, QT, 512), BF),
            vm((4, 2, QT, 512), BF),
            vm((4, QT, 512), BF),
            pltpu.SemaphoreType.DMA((6,)),
            pltpu.SemaphoreType.DMA((4,)),
            pltpu.SemaphoreType.DMA((N_COPIES,)),
            pltpu.SemaphoreType.DMA((N_COPIES,)),
        ],
        compiler_params=pltpu.CompilerParams(
            collective_id=0, has_side_effects=True, vmem_limit_bytes=60 * 2**20
        ),
        cost_estimate=pl.CostEstimate(
            flops=8 * 10**9, bytes_accessed=8 * 2**20, transcendentals=2**22
        ),
    )(states, w_query, w_output, kv_store, rows)


def local(states, w_query, w_output, kv_store, neighbour_ids, block_row):
    ids = neighbour_ids[:, :, None]
    cols = jnp.arange(block_row.shape[0], dtype=jnp.int32)
    rows = jnp.sum(jnp.where(ids == cols, block_row, 0), axis=2)
    rows = jnp.pad(rows, ((0, 0), (0, 126)))
    mixed = exchange(states, w_query, w_output, kv_store, rows)
    keep = T - STRETCH + 1
    trailing = lax.ppermute(mixed[keep:], "seq", [(i, i + 1) for i in range(NSEQ - 1)])
    return jnp.concatenate([trailing, mixed[:keep]], axis=0)


def solution(mesh):
    in_specs = (
        P("seq", None),
        P("seq", "head"),
        P("head", "seq"),
        P("seq", None, None, "head"),
        P("seq", None),
        P(),
    )
    out_specs = P("seq", "head")
    return jax.shard_map(local, mesh=mesh, in_specs=in_specs, out_specs=out_specs, check_vma=False)
```

```python
import jax
import jax.numpy as jnp
from jax import lax
from jax.experimental import pallas as pl
from jax.experimental.pallas import tpu as pltpu
from jax.sharding import PartitionSpec as P

HD = 128
STRETCH = 64
NB_TOK = 128
NX, NZ, NY = 4, 8, 4
NSEQ, NHEAD = NX * NZ, 2 * NY
T = 512
W = 512
QT = 128
NEG = -1e30
SCALE = 1.0 / HD**0.5
MESH = pl.DeviceIdType.MESH
N_COPIES = 192
BF = jnp.bfloat16
F32 = jnp.float32


def quarter(i):
    return pl.ds(i * QT, QT)


def part(i):
    return pl.ds(pl.multiple_of(i * QT, QT), QT)


def kernel(
    states, wq, wo, kv, ids, table, out,
    st, wqg, acc, qall, kvr, oatt, ml, ro, sw, rw, wog, iall, ism,
    ctx, ps, pr, tf, t2s, t2r, t1s, t1r, kraw, fin, edge_s, edge_r, ost, lsem, osem, ssem, rsem,
):
    s, h = lax.axis_index("seq"), lax.axis_index("head")
    z, x, y, c = s // NX, s % NX, h // 2, h % 2
    up, down = (s + NX) % NSEQ, (s + NSEQ - NX) % NSEQ
    right, left = z * NX + (x + 1) % NX, z * NX + (x + NX - 1) % NX
    after, before = (s + 1) % NSEQ, (s + NSEQ - 1) % NSEQ
    yup, ydown, twin = (h + 2) % NHEAD, (h + NHEAD - 2) % NHEAD, h + 1 - 2 * c
    count = [0]
    started = {}

    def send(src, dst, seq=None, head=None):
        n = count[0]
        count[0] += 1
        copy = pltpu.make_async_remote_copy(
            src_ref=src,
            dst_ref=dst,
            send_sem=ssem.at[n],
            recv_sem=rsem.at[n],
            device_id=(s if seq is None else seq, h if head is None else head),
            device_id_type=MESH,
        )
        copy.start()
        started[id(copy)] = copy
        return copy

    barrier = pltpu.get_barrier_semaphore()
    peers = [((s + NX * i) % NSEQ, h) for i in range(1, NZ)]
    peers += [(right, h), (left, h), (after, h), (before, h)]
    peers += [(s, (h + i) % NHEAD) for i in range(1, NHEAD)]
    for peer in peers:
        pl.semaphore_signal(barrier, inc=1, device_id=peer, device_id_type=MESH)

    own = [
        pltpu.make_async_copy(states, st.at[pl.ds(0, T)], lsem.at[0]),
        pltpu.make_async_copy(wq, wqg.at[0, part(x)], lsem.at[1]),
        pltpu.make_async_copy(wo, wog.at[z, x], lsem.at[2]),
        pltpu.make_async_copy(kv.at[:, 1], kvr.at[pl.ds(x * 8, 8), 1], lsem.at[3]),
        pltpu.make_async_copy(ids, iall.at[0], lsem.at[4]),
        pltpu.make_async_copy(kv.at[:, 0], kraw, lsem.at[6]),
    ]
    for i in (5, 3, 1, 0, 2, 4):
        own[i].start()

    own[5].wait()

    def turn_keys(b, _):
        for i in range(W // HD):
            cols = slice(i * HD, i * HD + HD)
            kvr[x * 8 + b, 0, :, cols] = jnp.transpose(kraw[b, :, cols])
        return 0

    lax.fori_loop(0, 8, turn_keys, 0)
    pl.semaphore_wait(barrier, len(peers))

    wx = {}
    wx[1] = send(wq, wqg.at[0, part(x)], seq=right)
    wx[3] = send(wq, wqg.at[0, part(x)], seq=left)
    wup, wdown = {}, {}

    def wsend(j, d, first=False):
        at = part((x + NX - d) % NX)
        src = wq if first else wqg.at[j, at]
        if j < 3 or (j == 3 and d in (0, 1)):
            wup[j + 1, d] = send(src, wqg.at[j + 1, at], seq=up)
        if j in (0, 7, 6) or (j == 5 and d in (2, 3)):
            wdown[(j + 7) % 8, d] = send(src, wqg.at[(j + 7) % 8, at], seq=down)

    wsend(0, 0, first=True)
    oup, odown = {}, {}

    def osend(step):
        if step == 1:
            oup[1] = send(wo, wog.at[z, x], seq=up)
            odown[1] = send(wo, wog.at[z, x], seq=down)
            return
        oup[step - 1].wait_recv()
        a = (z + NZ - step + 1) % NZ
        if step < 4:
            oup[step] = send(wog.at[a, x], wog.at[a, x], seq=up)
        else:
            half = pl.ds(0, 256)
            oup[step] = send(wog.at[a, x, half], wog.at[a, x, half], seq=up)
        odown[step - 1].wait_recv()
        b = (z + step - 1) % NZ
        if step < 4:
            odown[step] = send(wog.at[b, x], wog.at[b, x], seq=down)
        else:
            half = pl.ds(256, 256)
            odown[step] = send(wog.at[b, x, half], wog.at[b, x, half], seq=down)

    osend(1)
    rids = [
        send(ids, iall.at[i], seq=(s + NX * i) % NSEQ) for i in range(1, NZ)
    ]
    hcols = pl.ds(pl.multiple_of(h * W, W), W)
    tail = st.at[pl.ds(T, 64), hcols]
    first_rows = send(states.at[pl.ds(0, 64), hcols], tail, seq=before)

    own[1].wait()
    wx[1].wait_recv()
    lo, hi = (x + 3) % NX, (x + 1) % NX
    halves = [
        wqg.at[0, pl.ds(pl.multiple_of(lo * QT, QT), 64)],
        wqg.at[0, pl.ds(pl.multiple_of(hi * QT + 64, 64), 64)],
    ]
    wx[2] = send(halves[0], halves[0], seq=right)
    wsend(0, 1)
    wx[3].wait_recv()
    wx[4] = send(halves[1], halves[1], seq=left)
    wsend(0, 3)

    own[3].wait()

    def blocks(xo, half):
        return kvr.at[pl.ds(xo * 8 + 4 * half, 4)]

    kvs = {}
    kvs["r0"] = send(blocks(x, 0), blocks(x, 0), seq=right)
    kvs["l1"] = send(blocks(x, 1), blocks(x, 1), seq=left)
    kvs["r1"] = send(blocks(x, 1), blocks(x, 1), seq=right)
    kvs["l0"] = send(blocks(x, 0), blocks(x, 0), seq=left)

    wx[2].wait_recv()
    wx[4].wait_recv()
    wsend(0, 2)

    first_rows.wait_recv()
    others = [send(tail, tail, head=(h + i) % NHEAD) for i in range(1, NHEAD)]
    osend(2)

    def multiply(j):
        cols = pl.ds(pl.multiple_of(((z + NZ - j) % NZ) * 512, 512), 512)

        def body(i, _):
            r = pl.ds(pl.multiple_of(i * 192, 64), 192)
            term = jnp.dot(st[r, cols], wqg[j], preferred_element_type=F32)
            acc[r, :] = term if j == 0 else acc[r, :] + term
            return 0

        lax.fori_loop(0, 3, body, 0)

    order = (0, 1, 3, 2)
    for j in (1, 2, 3):
        for d in order:
            wup[j, d].wait_recv()
            wdown[8 - j, d].wait_recv()
            wsend(j, d)
            wsend(8 - j, d)
        if j == 1:
            own[0].wait()
            for copy in others:
                copy.wait_recv()
            for copy in others:
                copy.wait_send()
                del started[id(copy)]

            @pl.when(s == NSEQ - 1)
            def _():
                st[pl.ds(T, 64), :] = jnp.zeros((64, NHEAD * W), BF)

            multiply(0)
        if j == 3:
            kvs["r0"].wait_recv()
            kvs["r2"] = send(blocks(lo, 0), blocks(lo, 0), seq=right)
            kvs["l1"].wait_recv()
            kvs["l2"] = send(blocks(hi, 1), blocks(hi, 1), seq=left)
        if j < 3:
            osend(j + 2)
        multiply(j)
        multiply(8 - j)
    for d in (0, 1):
        wup[4, d].wait_recv()
    for d in (2, 3):
        wdown[4, d].wait_recv()
    multiply(4)

    qup, qdown = {}, {}

    def qsend(j, q):
        at = qall.at[j, quarter(q)]
        if j < 3 or (j == 3 and q < 2):
            qup[j + 1, q] = send(at, qall.at[j + 1, quarter(q)], seq=up)
        if j in (0, 7, 6) or (j == 5 and q >= 2):
            k = (j + 7) % 8
            qdown[k, q] = send(at, qall.at[k, quarter(q)], seq=down)

    for q in range(4):
        qall[0, quarter(q), :] = acc[pl.ds(63 + q * QT, QT), :].astype(BF)
        qsend(0, q)

    for copy in rids:
        copy.wait_recv()
    own[4].wait()
    scalars = pltpu.make_async_copy(iall, ism, lsem.at[5])
    scalars.start()
    oup[4].wait_recv()
    odown[4].wait_recv()
    scalars.wait()

    for j in (1, 2):
        for q in range(4):
            qup[j, q].wait_recv()
            qdown[8 - j, q].wait_recv()
            qsend(j, q)
            qsend(8 - j, q)

    for name in ("r1", "l0", "r2", "l2"):
        kvs[name].wait_recv()

    own[2].wait()
    oxs = {}
    oxs["r"] = send(wog.at[:, x], wog.at[:, x], seq=right)
    oxs["l"] = send(wog.at[:, x], wog.at[:, x], seq=left)

    lane = lax.broadcasted_iota(jnp.int32, (STRETCH, 128), 1)
    wide = lax.broadcasted_iota(jnp.int32, (1, 2 * NB_TOK), 1)

    def attend(j, g):
        r0, r1 = table[ism[j, 0, g]], table[ism[j, 1, g]]
        off0 = jnp.where(r0 // 32 == z, 0.0, NEG)
        off1 = jnp.where(r1 // 32 == z, 0.0, NEG)
        bias = jnp.where(wide < NB_TOK, off0, off1)
        b0, b1 = r0 % 32, r1 % 32
        at = pl.ds(pl.multiple_of(g * STRETCH, STRETCH), STRETCH)
        stats = jnp.zeros((STRETCH, 128), F32)
        for i in range(W // HD):
            cols = slice(i * HD, i * HD + HD)
            keys = jnp.concatenate([kvr[b0, 0, :, cols], kvr[b1, 0, :, cols]], axis=1)
            scores = jnp.dot(qall[j, at, cols], keys, preferred_element_type=F32)
            scores = scores * SCALE + bias
            top = jnp.max(scores, axis=1, keepdims=True)
            weights = jnp.exp(scores - top).astype(BF)
            total = jnp.sum(weights.astype(F32), axis=1, keepdims=True)
            values = jnp.concatenate([kvr[b0, 1, :, cols], kvr[b1, 1, :, cols]], axis=0)
            got = jnp.dot(weights, values, preferred_element_type=F32)
            oatt[j, at, cols] = got.astype(BF)
            stats = jnp.where(lane == i, top, jnp.where(lane == i + 4, total, stats))
        ml[j, at, :] = stats

    def attend_slots(a, b):
        def body(i, _):
            for g in range(4):
                attend(jnp.where(i < 2, a, b), (i % 2) * 4 + g)
            return 0

        lax.fori_loop(0, 2 if a == b else 4, body, 0)

    attend_slots(1, 7)
    for q in range(4):
        if q < 2:
            qup[3, q].wait_recv()
            qsend(3, q)
        else:
            qdown[5, q].wait_recv()
            qsend(5, q)
    attend_slots(2, 6)
    for q in range(4):
        if q < 2:
            qdown[5, q].wait_recv()
        else:
            qup[3, q].wait_recv()
    attend_slots(3, 5)
    for q in range(4):
        (qup if q < 2 else qdown)[4, q].wait_recv()
    attend_slots(4, 4)

    sent, sent_stats = {}, {}

    def rsend(way, k, q, rows_at):
        j = k if way == 0 else 8 - k
        there = down if way == 0 else up
        sent[way, k, q] = send(oatt.at[j, rows_at], ro.at[way, k - 1, rows_at], seq=there)
        sent_stats[way, k, q] = send(sw.at[j, q], rw.at[way, k - 1, q], seq=there)

    def turn_out(j, q):
        sw[j, q] = jnp.transpose(ml[j, quarter(q), :])[0:8, :]

    def turn_in(way, k, q):
        wire = jnp.concatenate([rw[way, k - 1, q], jnp.zeros((120, 128), F32)], axis=0)
        return jnp.transpose(wire)

    def merge(way, k, q, start, size):
        j = k if way == 0 else 8 - k
        at = pl.ds(q * QT + start, size)
        a = turn_in(way, k + 1, q)[start : start + size]
        b = ml[j, at, :]
        top = jnp.maximum(a, b)
        ea, eb = jnp.exp(a - top), jnp.exp(b - top)
        total = a * pltpu.roll(ea, 4, axis=1) + b * pltpu.roll(eb, 4, axis=1)
        lanes = lax.broadcasted_iota(jnp.int32, (size, 128), 1)
        ml[j, at, :] = jnp.where(lanes < 4, top, jnp.where(lanes < 8, total, 0.0))
        for i in range(W // HD):
            cols = slice(i * HD, i * HD + HD)
            mixed = ea[:, i : i + 1] * ro[way, k, at, cols].astype(F32)
            mixed = mixed + eb[:, i : i + 1] * oatt[j, at, cols].astype(F32)
            oatt[j, at, cols] = mixed.astype(BF)

    def weights_for(g):
        return jnp.concatenate([wog[g, i] for i in range(NX)], axis=1)

    def join(q):
        at = quarter(q)
        for way in (0, 1):
            sent[way, 1, q].wait_recv()
            sent_stats[way, 1, q].wait_recv()
        a, b, e = turn_in(0, 1, q), turn_in(1, 1, q), ml[0, at, :]
        top = jnp.maximum(jnp.maximum(a, b), e)
        fa, fb, fe = jnp.exp(a - top), jnp.exp(b - top), jnp.exp(e - top)
        total = a * pltpu.roll(fa, 4, axis=1) + b * pltpu.roll(fb, 4, axis=1)
        total = total + e * pltpu.roll(fe, 4, axis=1)
        total = pltpu.roll(total, 124, axis=1)
        fa, fb, fe = fa / total, fb / total, fe / total
        for i in range(W // HD):
            cols = slice(i * HD, i * HD + HD)
            mixed = fa[:, i : i + 1] * ro[0, 0, at, cols].astype(F32)
            mixed = mixed + fb[:, i : i + 1] * ro[1, 0, at, cols].astype(F32)
            mixed = mixed + fe[:, i : i + 1] * oatt[0, at, cols].astype(F32)
            ctx[q, :, cols] = mixed.astype(BF)

    pairs, seconds, thirds, written = {}, {}, {}, []

    def for_twin(q):
        def body(i, _):
            g = 2 * ((y + i) % NY) + 1 - c
            ps[q, i] = jnp.dot(ctx[q], weights_for(g), preferred_element_type=F32).astype(BF)
            return 0

        lax.fori_loop(0, NY, body, 0)
        pairs[q] = send(ps.at[q], pr.at[q], head=twin)

    def for_self(q):
        pairs[q].wait_recv()

        def body(i, _):
            g = 2 * ((y + i) % NY) + c
            term = jnp.dot(ctx[q], weights_for(g), preferred_element_type=F32)
            tf[q, i] = term + pr[q, i].astype(F32)
            return 0

        lax.fori_loop(0, NY, body, 0)
        t2s[q] = tf[q, 2].astype(BF)
        a, b = pl.ds(0, 64), pl.ds(64, 64)
        seconds[q] = (
            send(t2s.at[q, a], t2r.at[q, a], head=yup),
            send(t2s.at[q, b], t2r.at[q, b], head=ydown),
        )

    def pass_on(q):
        for copy in seconds[q]:
            copy.wait_recv()
        t1s[q, 0, 0:64] = (tf[q, 1, 0:64] + t2r[q, 0:64].astype(F32)).astype(BF)
        t1s[q, 0, 64:128] = tf[q, 1, 64:128].astype(BF)
        t1s[q, 1, 0:64] = tf[q, 3, 0:64].astype(BF)
        t1s[q, 1, 64:128] = (tf[q, 3, 64:128] + t2r[q, 64:128].astype(F32)).astype(BF)
        thirds[q] = (
            send(t1s.at[q, 0], t1r.at[q, 0], head=yup),
            send(t1s.at[q, 1], t1r.at[q, 1], head=ydown),
        )

    def finish(q):
        for copy in thirds[q]:
            copy.wait_recv()
        total = tf[q, 0] + t1r[q, 0].astype(F32) + t1r[q, 1].astype(F32)
        fin[pl.ds(64 + q * QT, QT), :] = total

    def give_edge():
        edge_s[...] = fin[pl.ds(T, 64), :].astype(BF)
        return send(edge_s, edge_r, seq=after)

    def take_edge(copy):
        copy.wait_recv()
        fin[pl.ds(0, 64), :] = jnp.where(s == 0, 0.0, edge_r[...].astype(F32))

    def write(i):
        ost[i] = fin[pl.ds(i * QT + 1, QT), :].astype(BF)
        copy = pltpu.make_async_copy(ost.at[i], out.at[quarter(i)], osem.at[i])
        copy.start()
        written.append(copy)

    def open_wave(q):
        turn_out(4, q)
        rsend(0, 4, q, pl.ds(q * QT, 64))
        rsend(1, 4, q, pl.ds(q * QT + 64, 64))

    def hop(k, q):
        for way in (0, 1):
            sent[way, k + 1, q].wait_recv()
            sent_stats[way, k + 1, q].wait_recv()
            if k == 3:
                merge(way, k, q, 64 * way, 64)
            else:
                merge(way, k, q, 0, QT)
            turn_out(k if way == 0 else 8 - k, q)
            rsend(way, k, q, quarter(q))

    for q in (3, 0):
        open_wave(q)
    for q in (3, 0):
        hop(3, q)
    attend_slots(0, 0)
    for q in (3, 0):
        hop(2, q)
    oxs["r"].wait_recv()
    lower = wog.at[pl.ds(0, 4), lo]
    oxs["r2"] = send(lower, lower, seq=right)
    oxs["l"].wait_recv()
    upper = wog.at[pl.ds(4, 4), hi]
    oxs["l2"] = send(upper, upper, seq=left)
    for q in (3, 0):
        hop(1, q)
    for q in (1, 2):
        open_wave(q)
    for q in (3, 0):
        join(q)
    for q in (1, 2):
        hop(3, q)
    for name in ("r2", "l2"):
        oxs[name].wait_recv()
    for q in (3, 0):
        for_twin(q)
    for q in (3, 0):
        for_self(q)
    for q in (1, 2):
        hop(2, q)
    for q in (3, 0):
        pass_on(q)
    for q in (1, 2):
        hop(1, q)
    finish(3)
    edge = give_edge()
    finish(0)
    take_edge(edge)
    write(0)
    join(1)
    for_twin(1)
    join(2)
    for_twin(2)
    for_self(1)
    for_self(2)
    pass_on(1)
    pass_on(2)
    finish(1)
    write(1)
    finish(2)
    write(2)
    write(3)
    for copy in written:
        copy.wait()
    for copy in started.values():
        copy.wait_send()


def exchange(states, w_query, w_output, kv_store, ids, table):
    anywhere = pl.BlockSpec(memory_space=pl.ANY)
    vm = pltpu.VMEM
    return pl.pallas_call(
        kernel,
        out_shape=jax.ShapeDtypeStruct((T, W), BF),
        in_specs=[anywhere] * 5 + [pl.BlockSpec(memory_space=pltpu.SMEM)],
        out_specs=anywhere,
        scratch_shapes=[
            vm((T + 64, NHEAD * W), BF),
            vm((NZ, 512, W), BF),
            vm((T + 64, W), F32),
            vm((NZ, T, W), BF),
            vm((32, 2, NB_TOK, W), BF),
            vm((NZ, T, W), BF),
            vm((NZ, T, 128), F32),
            vm((2, 4, T, W), BF),
            vm((NZ, 4, 8, 128), F32),
            vm((2, 4, 4, 8, 128), F32),
            vm((NZ, NX, W, 128), BF),
            vm((NZ, 2, 8), jnp.int32),
            pltpu.SMEM((NZ, 2, 8), jnp.int32),
            vm((4, QT, W), BF),
            vm((4, NY, QT, 512), BF),
            vm((4, NY, QT, 512), BF),
            vm((4, NY, QT, 512), F32),
            vm((4, QT, 512), BF),
            vm((4, QT, 512), BF),
            vm((4, 2, QT, 512), BF),
            vm((4, 2, QT, 512), BF),
            vm((8, NB_TOK, W), BF),
            vm((T + 64, W), F32),
            vm((64, W), BF),
            vm((64, W), BF),
            vm((4, QT, 512), BF),
            pltpu.SemaphoreType.DMA((8,)),
            pltpu.SemaphoreType.DMA((4,)),
            pltpu.SemaphoreType.DMA((N_COPIES,)),
            pltpu.SemaphoreType.DMA((N_COPIES,)),
        ],
        compiler_params=pltpu.CompilerParams(
            collective_id=0, has_side_effects=True, vmem_limit_bytes=60 * 2**20
        ),
        cost_estimate=pl.CostEstimate(
            flops=8 * 10**9, bytes_accessed=8 * 2**20, transcendentals=2**22
        ),
    )(states, w_query, w_output, kv_store, ids, table)


def local(states, w_query, w_output, kv_store, neighbour_ids, block_row):
    return exchange(states, w_query, w_output, kv_store, neighbour_ids.T, block_row)


def solution(mesh):
    in_specs = (
        P("seq", None),
        P("seq", "head"),
        P("head", "seq"),
        P("seq", None, None, "head"),
        P("seq", None),
        P(),
    )
    out_specs = P("seq", "head")
    return jax.shard_map(local, mesh=mesh, in_specs=in_specs, out_specs=out_specs, check_vma=False)
```

```python
import jax
import jax.numpy as jnp
from jax import lax
from jax.experimental import pallas as pl
from jax.experimental.pallas import tpu as pltpu
from jax.sharding import PartitionSpec as P

HD = 128
STRETCH = 64
NB_TOK = 128
NX, NZ, NY = 4, 8, 4
NSEQ, NHEAD = NX * NZ, 2 * NY
T = 512
W = 512
QT = 128
NEG = -1e30
SCALE = 1.0 / HD**0.5
MESH = pl.DeviceIdType.MESH
N_COPIES = 232
PA, PB = 80, 48
BF = jnp.bfloat16
F32 = jnp.float32


def quarter(i):
    return pl.ds(i * QT, QT)


def part(i):
    return pl.ds(pl.multiple_of(i * QT, QT), QT)


def kernel(
    states, wq, wo, kv, ids, table, out,
    st, wqg, acc, qall, kvr, oatt, ml, ro, sw, rw, wog, iall, ism,
    ctx, ps, pr, tf, t2s, t2r, t1s, t1r, kraw, fin, edge_s, edge_r, ost, lsem, osem, ssem, rsem,
):
    s, h = lax.axis_index("seq"), lax.axis_index("head")
    z, x, y, c = s // NX, s % NX, h // 2, h % 2
    up, down = (s + NX) % NSEQ, (s + NSEQ - NX) % NSEQ
    right, left = z * NX + (x + 1) % NX, z * NX + (x + NX - 1) % NX
    after, before = (s + 1) % NSEQ, (s + NSEQ - 1) % NSEQ
    yup, ydown, twin = (h + 2) % NHEAD, (h + NHEAD - 2) % NHEAD, h + 1 - 2 * c
    count = [0]
    started = {}

    def send(src, dst, seq=None, head=None):
        n = count[0]
        count[0] += 1
        copy = pltpu.make_async_remote_copy(
            src_ref=src,
            dst_ref=dst,
            send_sem=ssem.at[n],
            recv_sem=rsem.at[n],
            device_id=(s if seq is None else seq, h if head is None else head),
            device_id_type=MESH,
        )
        copy.start()
        started[id(copy)] = copy
        return copy

    barrier = pltpu.get_barrier_semaphore()
    peers = [((s + NX * i) % NSEQ, h) for i in range(1, NZ)]
    peers += [(right, h), (left, h), (after, h), (before, h)]
    peers += [(s, (h + i) % NHEAD) for i in range(1, NHEAD)]
    for peer in peers:
        pl.semaphore_signal(barrier, inc=1, device_id=peer, device_id_type=MESH)

    own = [
        pltpu.make_async_copy(states, st.at[pl.ds(0, T)], lsem.at[0]),
        pltpu.make_async_copy(wq, wqg.at[0, part(x)], lsem.at[1]),
        pltpu.make_async_copy(wo, wog.at[z, x], lsem.at[2]),
        pltpu.make_async_copy(kv.at[:, 1], kvr.at[pl.ds(x * 8, 8), 1], lsem.at[3]),
        pltpu.make_async_copy(ids, iall.at[0], lsem.at[4]),
        pltpu.make_async_copy(kv.at[:, 0], kraw, lsem.at[6]),
    ]
    for i in (5, 3, 1, 0, 2, 4):
        own[i].start()

    pl.semaphore_wait(barrier, len(peers))

    def arows(d, start=0, size=PA):
        return pl.ds(pl.multiple_of(((x + NX - d) % NX) * QT + start, 16), size)

    def brows(xo, start=0, size=PB):
        return pl.ds(pl.multiple_of(xo * QT + PA + start, 16), size)

    wx, bup, bdown = {}, {}, {}
    wup, wdown = {}, {}

    def bsend(step):
        src = wq.at[pl.ds(PA, PB)]
        if step == 1:
            bup[1] = send(src, wqg.at[1, brows(x)], seq=up)
            bdown[1] = send(src, wqg.at[7, brows(x)], seq=down)
            return
        at = brows(x) if step < 4 else brows(x, 0, 32)
        bup[step - 1].wait_recv()
        bup[step] = send(wqg.at[step - 1, at], wqg.at[step, at], seq=up)
        at = brows(x) if step < 4 else brows(x, 32, 16)
        bdown[step - 1].wait_recv()
        bdown[step] = send(wqg.at[9 - step, at], wqg.at[8 - step, at], seq=down)

    def wsend(j, d, first=False):
        at = arows(d)
        src = wq.at[pl.ds(0, PA)] if first else wqg.at[j, at]
        if j < 3 or (j == 3 and d in (0, 1)):
            wup[j + 1, d] = send(src, wqg.at[j + 1, at], seq=up)
        if j in (0, 7, 6) or (j == 5 and d in (2, 3)):
            wdown[(j + 7) % 8, d] = send(src, wqg.at[(j + 7) % 8, at], seq=down)

    wx[1] = send(wq.at[pl.ds(0, PA)], wqg.at[0, arows(0)], seq=right)
    wx[3] = send(wq.at[pl.ds(0, PA)], wqg.at[0, arows(0)], seq=left)
    bsend(1)
    wsend(0, 0, first=True)

    own[5].wait()

    def turn_keys(b, _):
        for i in range(W // HD):
            cols = slice(i * HD, i * HD + HD)
            kvr[x * 8 + b, 0, :, cols] = jnp.transpose(kraw[b, :, cols])
        return 0

    lax.fori_loop(0, 8, turn_keys, 0)
    wx[1].wait_recv()
    wx[2] = send(wqg.at[0, arows(1, 0, 48)], wqg.at[0, arows(1, 0, 48)], seq=right)
    wx[3].wait_recv()
    wx[4] = send(wqg.at[0, arows(3, 48, 32)], wqg.at[0, arows(3, 48, 32)], seq=left)
    bsend(2)
    wsend(0, 1)
    wsend(0, 3)
    iids = [send(ids, iall.at[i], seq=(s + NX * i) % NSEQ) for i in range(1, NZ)]
    hcols = pl.ds(pl.multiple_of(h * W, W), W)
    tail = st.at[pl.ds(T, 64), hcols]
    first_rows = send(states.at[pl.ds(0, 64), hcols], tail, seq=before)
    bsend(3)

    lo, hi = (x + 3) % NX, (x + 1) % NX
    kvright, kvleft = {}, {}
    own[3].wait()

    def kvsend(n):
        a, b = n % 8, (n + 4) % 8
        if n < 8:
            xa, xb = x, x
        else:
            xa, xb = lo, hi
            kvright[n - 8].wait_recv()
            kvleft[n - 8].wait_recv()
        kvright[n] = send(kvr.at[xa * 8 + a], kvr.at[xa * 8 + a], seq=right)
        kvleft[n] = send(kvr.at[xb * 8 + b], kvr.at[xb * 8 + b], seq=left)

    kvsend(0)
    wx[2].wait_recv()
    wx[4].wait_recv()
    wsend(0, 2)
    bsend(4)
    kvsend(1)
    first_rows.wait_recv()
    others = [send(tail, tail, head=(h + i) % NHEAD) for i in range(1, NHEAD)]
    own[1].wait()
    bup[4].wait_recv()
    bdown[4].wait_recv()
    bx = {}
    bx["r"] = send(wqg.at[:, brows(x)], wqg.at[:, brows(x)], seq=right)
    bx["l"] = send(wqg.at[:, brows(x)], wqg.at[:, brows(x)], seq=left)
    kvsend(2)

    oup, odown = {}, {}

    def osend(step):
        if step == 1:
            oup[1] = send(wo, wog.at[z, x], seq=up)
            odown[1] = send(wo, wog.at[z, x], seq=down)
            return
        oup[step - 1].wait_recv()
        a = (z + NZ - step + 1) % NZ
        if step < 4:
            oup[step] = send(wog.at[a, x], wog.at[a, x], seq=up)
        else:
            half = pl.ds(0, 256)
            oup[step] = send(wog.at[a, x, half], wog.at[a, x, half], seq=up)
        odown[step - 1].wait_recv()
        b = (z + step - 1) % NZ
        if step < 4:
            odown[step] = send(wog.at[b, x], wog.at[b, x], seq=down)
        else:
            half = pl.ds(256, 256)
            odown[step] = send(wog.at[b, x, half], wog.at[b, x, half], seq=down)

    def multiply(j):
        cols = pl.ds(pl.multiple_of(((z + NZ - j) % NZ) * 512, 512), 512)

        def body(i, _):
            r = pl.ds(pl.multiple_of(i * 192, 64), 192)
            term = jnp.dot(st[r, cols], wqg[j], preferred_element_type=F32)
            acc[r, :] = term if j == 0 else acc[r, :] + term
            return 0

        lax.fori_loop(0, 3, body, 0)

    order = (0, 1, 3, 2)
    for j in (1, 2, 3):
        for d in order:
            wup[j, d].wait_recv()
            wdown[8 - j, d].wait_recv()
            wsend(j, d)
            wsend(8 - j, d)
        if j == 1:
            osend(1)
            bx["r"].wait_recv()
            at = (pl.ds(0, 4), brows(lo))
            bx["r2"] = send(wqg.at[at], wqg.at[at], seq=right)
            bx["l"].wait_recv()
            at = (pl.ds(4, 4), brows(hi))
            bx["l2"] = send(wqg.at[at], wqg.at[at], seq=left)
            kvsend(3)
        if j == 2:
            osend(2)
            kvsend(4)
            kvsend(5)
            own[0].wait()
            for copy in others:
                copy.wait_recv()
            for copy in others:
                copy.wait_send()
                del started[id(copy)]

            @pl.when(s == NSEQ - 1)
            def _():
                st[pl.ds(T, 64), :] = jnp.zeros((64, NHEAD * W), BF)

        if j == 3:
            osend(3)
            kvsend(6)
            kvsend(7)
            bx["r2"].wait_recv()
            bx["l2"].wait_recv()
            for n in (0, 1, 7, 2, 6, 3, 5):
                multiply(n)
    for d in (0, 1):
        wup[4, d].wait_recv()
    for d in (2, 3):
        wdown[4, d].wait_recv()
    multiply(4)

    qup, qdown = {}, {}

    def qsend(j, q):
        at = qall.at[j, quarter(q)]
        if j < 3 or (j == 3 and q < 2):
            qup[j + 1, q] = send(at, qall.at[j + 1, quarter(q)], seq=up)
        if j in (0, 7, 6) or (j == 5 and q >= 2):
            k = (j + 7) % 8
            qdown[k, q] = send(at, qall.at[k, quarter(q)], seq=down)

    for q in range(4):
        qall[0, quarter(q), :] = acc[pl.ds(63 + q * QT, QT), :].astype(BF)
        qsend(0, q)

    kvsend(8)
    kvsend(9)
    for copy in iids:
        copy.wait_recv()
    own[4].wait()
    scalars = pltpu.make_async_copy(iall, ism, lsem.at[5])
    scalars.start()
    scalars.wait()

    for j in (1, 2):
        for q in range(4):
            qup[j, q].wait_recv()
            qdown[8 - j, q].wait_recv()
            qsend(j, q)
            qsend(8 - j, q)
        if j == 1:
            osend(4)
            kvsend(10)
            kvsend(11)

    for n in range(4, 12):
        kvright[n].wait_recv()
        kvleft[n].wait_recv()
    oup[4].wait_recv()
    odown[4].wait_recv()

    own[2].wait()
    oxs = {}
    oxs["r"] = send(wog.at[:, x], wog.at[:, x], seq=right)
    oxs["l"] = send(wog.at[:, x], wog.at[:, x], seq=left)

    lane = lax.broadcasted_iota(jnp.int32, (STRETCH, 128), 1)
    wide = lax.broadcasted_iota(jnp.int32, (1, 2 * NB_TOK), 1)

    def attend(j, g):
        r0, r1 = table[ism[j, 0, g]], table[ism[j, 1, g]]
        off0 = jnp.where(r0 // 32 == z, 0.0, NEG)
        off1 = jnp.where(r1 // 32 == z, 0.0, NEG)
        bias = jnp.where(wide < NB_TOK, off0, off1)
        b0, b1 = r0 % 32, r1 % 32
        at = pl.ds(pl.multiple_of(g * STRETCH, STRETCH), STRETCH)
        stats = jnp.zeros((STRETCH, 128), F32)
        for i in range(W // HD):
            cols = slice(i * HD, i * HD + HD)
            keys = jnp.concatenate([kvr[b0, 0, :, cols], kvr[b1, 0, :, cols]], axis=1)
            scores = jnp.dot(qall[j, at, cols], keys, preferred_element_type=F32)
            scores = scores * SCALE + bias
            top = jnp.max(scores, axis=1, keepdims=True)
            weights = jnp.exp(scores - top).astype(BF)
            total = jnp.sum(weights.astype(F32), axis=1, keepdims=True)
            values = jnp.concatenate([kvr[b0, 1, :, cols], kvr[b1, 1, :, cols]], axis=0)
            got = jnp.dot(weights, values, preferred_element_type=F32)
            oatt[j, at, cols] = got.astype(BF)
            stats = jnp.where(lane == i, top, jnp.where(lane == i + 4, total, stats))
        ml[j, at, :] = stats

    def attend_slots(a, b):
        def body(i, _):
            for g in range(4):
                attend(jnp.where(i < 2, a, b), (i % 2) * 4 + g)
            return 0

        lax.fori_loop(0, 2 if a == b else 4, body, 0)

    attend_slots(1, 7)
    for q in range(4):
        if q < 2:
            qup[3, q].wait_recv()
            qsend(3, q)
        else:
            qdown[5, q].wait_recv()
            qsend(5, q)
    attend_slots(2, 6)
    for q in range(4):
        if q < 2:
            qdown[5, q].wait_recv()
        else:
            qup[3, q].wait_recv()
    attend_slots(3, 5)
    for q in range(4):
        (qup if q < 2 else qdown)[4, q].wait_recv()
    attend_slots(4, 4)

    sent, sent_stats = {}, {}

    def rsend(way, k, q, rows_at):
        j = k if way == 0 else 8 - k
        there = down if way == 0 else up
        sent[way, k, q] = send(oatt.at[j, rows_at], ro.at[way, k - 1, rows_at], seq=there)
        sent_stats[way, k, q] = send(sw.at[j, q], rw.at[way, k - 1, q], seq=there)

    def turn_out(j, q):
        sw[j, q] = jnp.transpose(ml[j, quarter(q), :])[0:8, :]

    def turn_in(way, k, q):
        wire = jnp.concatenate([rw[way, k - 1, q], jnp.zeros((120, 128), F32)], axis=0)
        return jnp.transpose(wire)

    def merge(way, k, q, start, size):
        j = k if way == 0 else 8 - k
        at = pl.ds(q * QT + start, size)
        a = turn_in(way, k + 1, q)[start : start + size]
        b = ml[j, at, :]
        top = jnp.maximum(a, b)
        ea, eb = jnp.exp(a - top), jnp.exp(b - top)
        total = a * pltpu.roll(ea, 4, axis=1) + b * pltpu.roll(eb, 4, axis=1)
        lanes = lax.broadcasted_iota(jnp.int32, (size, 128), 1)
        ml[j, at, :] = jnp.where(lanes < 4, top, jnp.where(lanes < 8, total, 0.0))
        for i in range(W // HD):
            cols = slice(i * HD, i * HD + HD)
            mixed = ea[:, i : i + 1] * ro[way, k, at, cols].astype(F32)
            mixed = mixed + eb[:, i : i + 1] * oatt[j, at, cols].astype(F32)
            oatt[j, at, cols] = mixed.astype(BF)

    def weights_for(g):
        return jnp.concatenate([wog[g, i] for i in range(NX)], axis=1)

    def join(q):
        at = quarter(q)
        for way in (0, 1):
            sent[way, 1, q].wait_recv()
            sent_stats[way, 1, q].wait_recv()
        a, b, e = turn_in(0, 1, q), turn_in(1, 1, q), ml[0, at, :]
        top = jnp.maximum(jnp.maximum(a, b), e)
        fa, fb, fe = jnp.exp(a - top), jnp.exp(b - top), jnp.exp(e - top)
        total = a * pltpu.roll(fa, 4, axis=1) + b * pltpu.roll(fb, 4, axis=1)
        total = total + e * pltpu.roll(fe, 4, axis=1)
        total = pltpu.roll(total, 124, axis=1)
        fa, fb, fe = fa / total, fb / total, fe / total
        for i in range(W // HD):
            cols = slice(i * HD, i * HD + HD)
            mixed = fa[:, i : i + 1] * ro[0, 0, at, cols].astype(F32)
            mixed = mixed + fb[:, i : i + 1] * ro[1, 0, at, cols].astype(F32)
            mixed = mixed + fe[:, i : i + 1] * oatt[0, at, cols].astype(F32)
            ctx[q, :, cols] = mixed.astype(BF)

    pairs, seconds, thirds, written = {}, {}, {}, []

    far_first = (2, 1, 3, 0)

    def for_twin(q):
        for i in far_first:
            g = 2 * ((y + i) % NY) + 1 - c
            ps[q, i] = jnp.dot(ctx[q], weights_for(g), preferred_element_type=F32).astype(BF)
            pairs[q, i] = send(ps.at[q, i], pr.at[q, i], head=twin)

    def for_self(q):
        for i in far_first:
            g = 2 * ((y + i) % NY) + c
            term = jnp.dot(ctx[q], weights_for(g), preferred_element_type=F32)
            pairs[q, i].wait_recv()
            term = term + pr[q, i].astype(F32)
            if i != 2:
                tf[q, i] = term
                continue
            t2s[q] = term.astype(BF)
            a, b = pl.ds(0, 64), pl.ds(64, 64)
            seconds[q] = (
                send(t2s.at[q, a], t2r.at[q, a], head=yup),
                send(t2s.at[q, b], t2r.at[q, b], head=ydown),
            )

    def pass_on(q):
        for copy in seconds[q]:
            copy.wait_recv()
        t1s[q, 0, 0:64] = (tf[q, 1, 0:64] + t2r[q, 0:64].astype(F32)).astype(BF)
        t1s[q, 0, 64:128] = tf[q, 1, 64:128].astype(BF)
        t1s[q, 1, 0:64] = tf[q, 3, 0:64].astype(BF)
        t1s[q, 1, 64:128] = (tf[q, 3, 64:128] + t2r[q, 64:128].astype(F32)).astype(BF)
        thirds[q] = (
            send(t1s.at[q, 0], t1r.at[q, 0], head=yup),
            send(t1s.at[q, 1], t1r.at[q, 1], head=ydown),
        )

    def finish(q):
        for copy in thirds[q]:
            copy.wait_recv()
        total = tf[q, 0] + t1r[q, 0].astype(F32) + t1r[q, 1].astype(F32)
        fin[pl.ds(64 + q * QT, QT), :] = total

    def give_edge():
        edge_s[...] = fin[pl.ds(T, 64), :].astype(BF)
        return send(edge_s, edge_r, seq=after)

    def take_edge(copy):
        copy.wait_recv()
        fin[pl.ds(0, 64), :] = jnp.where(s == 0, 0.0, edge_r[...].astype(F32))

    def write(i):
        ost[i] = fin[pl.ds(i * QT + 1, QT), :].astype(BF)
        copy = pltpu.make_async_copy(ost.at[i], out.at[quarter(i)], osem.at[i])
        copy.start()
        written.append(copy)

    def open_wave(q):
        turn_out(4, q)
        rsend(0, 4, q, pl.ds(q * QT, 64))
        rsend(1, 4, q, pl.ds(q * QT + 64, 64))

    def hop(k, q):
        for way in (0, 1):
            sent[way, k + 1, q].wait_recv()
            sent_stats[way, k + 1, q].wait_recv()
            if k == 3:
                merge(way, k, q, 64 * way, 64)
            else:
                merge(way, k, q, 0, QT)
            turn_out(k if way == 0 else 8 - k, q)
            rsend(way, k, q, quarter(q))

    for q in (3, 0):
        open_wave(q)
    for q in (3, 0):
        hop(3, q)
    attend_slots(0, 0)
    for q in (3, 0):
        hop(2, q)
    oxs["r"].wait_recv()
    lower = wog.at[pl.ds(0, 4), lo]
    oxs["r2"] = send(lower, lower, seq=right)
    oxs["l"].wait_recv()
    upper = wog.at[pl.ds(4, 4), hi]
    oxs["l2"] = send(upper, upper, seq=left)
    for q in (3, 0):
        hop(1, q)
    for q in (1, 2):
        open_wave(q)
    for q in (3, 0):
        join(q)
    for q in (1, 2):
        hop(3, q)
    for name in ("r2", "l2"):
        oxs[name].wait_recv()
    for q in (3, 0):
        for_twin(q)
    for q in (3, 0):
        for_self(q)
    for q in (1, 2):
        hop(2, q)
    for q in (3, 0):
        pass_on(q)
    for q in (1, 2):
        hop(1, q)
    finish(3)
    edge = give_edge()
    finish(0)
    join(1)
    for_twin(1)
    join(2)
    for_twin(2)
    for_self(1)
    for_self(2)
    take_edge(edge)
    write(0)
    pass_on(1)
    pass_on(2)
    finish(1)
    write(1)
    finish(2)
    write(2)
    write(3)
    for copy in written:
        copy.wait()
    for copy in started.values():
        copy.wait_send()


def exchange(states, w_query, w_output, kv_store, ids, table):
    anywhere = pl.BlockSpec(memory_space=pl.ANY)
    vm = pltpu.VMEM
    return pl.pallas_call(
        kernel,
        out_shape=jax.ShapeDtypeStruct((T, W), BF),
        in_specs=[anywhere] * 5 + [pl.BlockSpec(memory_space=pltpu.SMEM)],
        out_specs=anywhere,
        scratch_shapes=[
            vm((T + 64, NHEAD * W), BF),
            vm((NZ, 512, W), BF),
            vm((T + 64, W), F32),
            vm((NZ, T, W), BF),
            vm((32, 2, NB_TOK, W), BF),
            vm((NZ, T, W), BF),
            vm((NZ, T, 128), F32),
            vm((2, 4, T, W), BF),
            vm((NZ, 4, 8, 128), F32),
            vm((2, 4, 4, 8, 128), F32),
            vm((NZ, NX, W, 128), BF),
            vm((NZ, 2, 8), jnp.int32),
            pltpu.SMEM((NZ, 2, 8), jnp.int32),
            vm((4, QT, W), BF),
            vm((4, NY, QT, 512), BF),
            vm((4, NY, QT, 512), BF),
            vm((4, NY, QT, 512), F32),
            vm((4, QT, 512), BF),
            vm((4, QT, 512), BF),
            vm((4, 2, QT, 512), BF),
            vm((4, 2, QT, 512), BF),
            vm((8, NB_TOK, W), BF),
            vm((T + 64, W), F32),
            vm((64, W), BF),
            vm((64, W), BF),
            vm((4, QT, 512), BF),
            pltpu.SemaphoreType.DMA((8,)),
            pltpu.SemaphoreType.DMA((4,)),
            pltpu.SemaphoreType.DMA((N_COPIES,)),
            pltpu.SemaphoreType.DMA((N_COPIES,)),
        ],
        compiler_params=pltpu.CompilerParams(
            collective_id=0, has_side_effects=True, vmem_limit_bytes=60 * 2**20
        ),
        cost_estimate=pl.CostEstimate(
            flops=8 * 10**9, bytes_accessed=8 * 2**20, transcendentals=2**22
        ),
    )(states, w_query, w_output, kv_store, ids, table)


def local(states, w_query, w_output, kv_store, neighbour_ids, block_row):
    return exchange(states, w_query, w_output, kv_store, neighbour_ids.T, block_row)


def solution(mesh):
    in_specs = (
        P("seq", None),
        P("seq", "head"),
        P("head", "seq"),
        P("seq", None, None, "head"),
        P("seq", None),
        P(),
    )
    out_specs = P("seq", "head")
    return jax.shard_map(local, mesh=mesh, in_specs=in_specs, out_specs=out_specs, check_vma=False)
```

```python
import jax
import jax.numpy as jnp
from jax import lax
from jax.experimental import pallas as pl
from jax.experimental.pallas import tpu as pltpu
from jax.sharding import PartitionSpec as P

HD = 128
STRETCH = 64
NB_TOK = 128
NX, NZ, NY = 4, 8, 4
NSEQ, NHEAD = NX * NZ, 2 * NY
T = 512
W = 512
QT = 128
NEG = -1e30
SCALE = 1.0 / HD**0.5
MESH = pl.DeviceIdType.MESH
N_COPIES = 232
PA, PB = 96, 32
AU, BU = (PA // 16 + 1) // 2 * 16, (PB // 16 + 1) // 2 * 16
BF = jnp.bfloat16
F32 = jnp.float32


def quarter(i):
    return pl.ds(i * QT, QT)


def part(i):
    return pl.ds(pl.multiple_of(i * QT, QT), QT)


def kernel(
    states, wq, wo, kv, ids, table, out,
    st, wqg, acc, qall, kv0, kv1, kv2, kv3, oatt, ml, ro, sw, rw, wog, iall, ism,
    ctx, ps, pr, tf, t2s, t2r, t1s, t1r, kraw, fin, edge_s, edge_r, ost, lsem, osem, ssem, rsem,
):
    s, h = lax.axis_index("seq"), lax.axis_index("head")
    z, x, y, c = s // NX, s % NX, h // 2, h % 2
    up, down = (s + NX) % NSEQ, (s + NSEQ - NX) % NSEQ
    right, left = z * NX + (x + 1) % NX, z * NX + (x + NX - 1) % NX
    after, before = (s + 1) % NSEQ, (s + NSEQ - 1) % NSEQ
    yup, ydown, twin = (h + 2) % NHEAD, (h + NHEAD - 2) % NHEAD, h + 1 - 2 * c
    kvh = (kv0, kv1, kv2, kv3)
    count = [0]
    started = {}

    def send(src, dst, seq=None, head=None):
        n = count[0]
        count[0] += 1
        copy = pltpu.make_async_remote_copy(
            src_ref=src,
            dst_ref=dst,
            send_sem=ssem.at[n],
            recv_sem=rsem.at[n],
            device_id=(s if seq is None else seq, h if head is None else head),
            device_id_type=MESH,
        )
        copy.start()
        started[id(copy)] = copy
        return copy

    barrier = pltpu.get_barrier_semaphore()
    peers = [((s + NX * i) % NSEQ, h) for i in range(1, NZ)]
    peers += [(right, h), (left, h), (after, h), (before, h)]
    peers += [(s, (h + i) % NHEAD) for i in range(1, NHEAD)]
    for peer in peers:
        pl.semaphore_signal(barrier, inc=1, device_id=peer, device_id_type=MESH)

    own = [
        pltpu.make_async_copy(states, st.at[pl.ds(0, T)], lsem.at[0]),
        pltpu.make_async_copy(wq, wqg.at[0, part(x)], lsem.at[1]),
        pltpu.make_async_copy(wo, wog.at[z, x], lsem.at[2]),
        pltpu.make_async_copy(ids, iall.at[0], lsem.at[3]),
        pltpu.make_async_copy(kv.at[:, 0], kraw, lsem.at[4]),
    ]
    own_values = [
        pltpu.make_async_copy(
            kv.at[:, 1, :, pl.ds(i * HD, HD)], kvh[i].at[pl.ds(x * 8, 8), 1], lsem.at[8 + i]
        )
        for i in range(4)
    ]
    own[4].start()
    for copy in own_values:
        copy.start()
    for i in (1, 0, 2, 3):
        own[i].start()

    pl.semaphore_wait(barrier, len(peers))

    def arows(d, start=0, size=PA):
        return pl.ds(pl.multiple_of(((x + NX - d) % NX) * QT + start, 16), size)

    def brows(xo, start=0, size=PB):
        return pl.ds(pl.multiple_of(xo * QT + PA + start, 16), size)

    wx, bup, bdown = {}, {}, {}
    wup, wdown = {}, {}

    def bsend(step):
        src = wq.at[pl.ds(PA, PB)]
        if step == 1:
            bup[1] = send(src, wqg.at[1, brows(x)], seq=up)
            bdown[1] = send(src, wqg.at[7, brows(x)], seq=down)
            return
        at = brows(x) if step < 4 else brows(x, 0, BU)
        bup[step - 1].wait_recv()
        bup[step] = send(wqg.at[step - 1, at], wqg.at[step, at], seq=up)
        at = brows(x) if step < 4 else brows(x, BU, PB - BU)
        bdown[step - 1].wait_recv()
        bdown[step] = send(wqg.at[9 - step, at], wqg.at[8 - step, at], seq=down)

    def wsend(j, d, first=False):
        at = arows(d)
        src = wq.at[pl.ds(0, PA)] if first else wqg.at[j, at]
        if j < 3 or (j == 3 and d in (0, 1)):
            wup[j + 1, d] = send(src, wqg.at[j + 1, at], seq=up)
        if j in (0, 7, 6) or (j == 5 and d in (2, 3)):
            wdown[(j + 7) % 8, d] = send(src, wqg.at[(j + 7) % 8, at], seq=down)

    wx[1] = send(wq.at[pl.ds(0, PA)], wqg.at[0, arows(0)], seq=right)
    wx[3] = send(wq.at[pl.ds(0, PA)], wqg.at[0, arows(0)], seq=left)
    bsend(1)
    wsend(0, 0, first=True)

    own[4].wait()

    def turn_keys(b, _):
        for i in range(W // HD):
            cols = slice(i * HD, i * HD + HD)
            kvh[i][x * 8 + b, 0] = jnp.transpose(kraw[b, :, cols])
        return 0

    lax.fori_loop(0, 8, turn_keys, 0)
    wx[1].wait_recv()
    wx[2] = send(wqg.at[0, arows(1, 0, AU)], wqg.at[0, arows(1, 0, AU)], seq=right)
    wx[3].wait_recv()
    wx[4] = send(wqg.at[0, arows(3, AU, PA - AU)], wqg.at[0, arows(3, AU, PA - AU)], seq=left)
    bsend(2)
    wsend(0, 1)
    wsend(0, 3)
    iids = [send(ids, iall.at[i], seq=(s + NX * i) % NSEQ) for i in range(1, NZ)]
    hcols = pl.ds(pl.multiple_of(h * W, W), W)
    tail = st.at[pl.ds(T, 64), hcols]
    first_rows = send(states.at[pl.ds(0, 64), hcols], tail, seq=before)
    bsend(3)

    lo, hi = (x + 3) % NX, (x + 1) % NX
    kvright, kvleft = {}, {}
    for copy in own_values:
        copy.wait()

    def blocks(i, xo, half):
        return kvh[i].at[pl.ds(xo * 8 + 4 * half, 4)]

    def kvsend(n):
        i, turn = n // 3, n % 3
        if turn < 2:
            a, b = blocks(i, x, turn), blocks(i, x, 1 - turn)
        else:
            a, b = blocks(i, lo, 0), blocks(i, hi, 1)
            kvright[3 * i].wait_recv()
            kvleft[3 * i].wait_recv()
        kvright[n] = send(a, a, seq=right)
        kvleft[n] = send(b, b, seq=left)

    def kvwait(i):
        for n in (3 * i + 1, 3 * i + 2):
            kvright[n].wait_recv()
            kvleft[n].wait_recv()

    kvsend(0)
    wx[2].wait_recv()
    wx[4].wait_recv()
    wsend(0, 2)
    bsend(4)
    kvsend(1)
    first_rows.wait_recv()
    others = [send(tail, tail, head=(h + i) % NHEAD) for i in range(1, NHEAD)]
    own[1].wait()
    bup[4].wait_recv()
    bdown[4].wait_recv()
    bx = {}
    bx["r"] = send(wqg.at[:, brows(x)], wqg.at[:, brows(x)], seq=right)
    bx["l"] = send(wqg.at[:, brows(x)], wqg.at[:, brows(x)], seq=left)
    kvsend(2)

    oup, odown = {}, {}

    def osend(step):
        if step == 1:
            oup[1] = send(wo, wog.at[z, x], seq=up)
            odown[1] = send(wo, wog.at[z, x], seq=down)
            return
        oup[step - 1].wait_recv()
        a = (z + NZ - step + 1) % NZ
        if step < 4:
            oup[step] = send(wog.at[a, x], wog.at[a, x], seq=up)
        else:
            half = pl.ds(0, 256)
            oup[step] = send(wog.at[a, x, half], wog.at[a, x, half], seq=up)
        odown[step - 1].wait_recv()
        b = (z + step - 1) % NZ
        if step < 4:
            odown[step] = send(wog.at[b, x], wog.at[b, x], seq=down)
        else:
            half = pl.ds(256, 256)
            odown[step] = send(wog.at[b, x, half], wog.at[b, x, half], seq=down)

    def multiply(j):
        cols = pl.ds(pl.multiple_of(((z + NZ - j) % NZ) * 512, 512), 512)

        def body(i, _):
            r = pl.ds(pl.multiple_of(i * 192, 64), 192)
            term = jnp.dot(st[r, cols], wqg[j], preferred_element_type=F32)
            acc[r, :] = term if j == 0 else acc[r, :] + term
            return 0

        lax.fori_loop(0, 3, body, 0)

    order = (0, 1, 3, 2)
    for j in (1, 2, 3):
        for d in order:
            wup[j, d].wait_recv()
            wdown[8 - j, d].wait_recv()
            wsend(j, d)
            wsend(8 - j, d)
        if j == 1:
            osend(1)
            bx["r"].wait_recv()
            at = (pl.ds(0, 4), brows(lo))
            bx["r2"] = send(wqg.at[at], wqg.at[at], seq=right)
            bx["l"].wait_recv()
            at = (pl.ds(4, 4), brows(hi))
            bx["l2"] = send(wqg.at[at], wqg.at[at], seq=left)
            kvsend(3)
        if j == 2:
            osend(2)
            kvsend(4)
            kvsend(6)
            own[0].wait()
            for copy in others:
                copy.wait_recv()
            for copy in others:
                copy.wait_send()
                del started[id(copy)]

            @pl.when(s == NSEQ - 1)
            def _():
                st[pl.ds(T, 64), :] = jnp.zeros((64, NHEAD * W), BF)

        if j == 3:
            osend(3)
            kvsend(5)
            kvsend(7)
            bx["r2"].wait_recv()
            bx["l2"].wait_recv()
            for n in (0, 1, 7, 2, 6, 3, 5):
                multiply(n)
    for d in (0, 1):
        wup[4, d].wait_recv()
    for d in (2, 3):
        wdown[4, d].wait_recv()
    multiply(4)

    qup, qdown = {}, {}

    def qsend(j, q):
        at = qall.at[j, quarter(q)]
        if j < 3 or (j == 3 and q < 2):
            qup[j + 1, q] = send(at, qall.at[j + 1, quarter(q)], seq=up)
        if j in (0, 7, 6) or (j == 5 and q >= 2):
            k = (j + 7) % 8
            qdown[k, q] = send(at, qall.at[k, quarter(q)], seq=down)

    for q in range(4):
        qall[0, quarter(q), :] = acc[pl.ds(63 + q * QT, QT), :].astype(BF)
        qsend(0, q)

    kvsend(9)
    for copy in iids:
        copy.wait_recv()
    own[3].wait()
    scalars = pltpu.make_async_copy(iall, ism, lsem.at[5])
    scalars.start()
    scalars.wait()

    lane = lax.broadcasted_iota(jnp.int32, (STRETCH, 128), 1)
    wide = lax.broadcasted_iota(jnp.int32, (1, 2 * NB_TOK), 1)

    def attend(j, g, i):
        r0, r1 = table[ism[j, 0, g]], table[ism[j, 1, g]]
        off0 = jnp.where(r0 // 32 == z, 0.0, NEG)
        off1 = jnp.where(r1 // 32 == z, 0.0, NEG)
        bias = jnp.where(wide < NB_TOK, off0, off1)
        b0, b1 = r0 % 32, r1 % 32
        at = pl.ds(g * STRETCH, STRETCH)
        cols = slice(i * HD, i * HD + HD)
        keys = jnp.concatenate([kvh[i][b0, 0], kvh[i][b1, 0]], axis=1)
        scores = jnp.dot(qall[j, at, cols], keys, preferred_element_type=F32)
        scores = scores * SCALE + bias
        top = jnp.max(scores, axis=1, keepdims=True)
        weights = jnp.exp(scores - top).astype(BF)
        total = jnp.sum(weights.astype(F32), axis=1, keepdims=True)
        values = jnp.concatenate([kvh[i][b0, 1], kvh[i][b1, 1]], axis=0)
        got = jnp.dot(weights, values, preferred_element_type=F32)
        oatt[j, at, cols] = got.astype(BF)
        stats = jnp.zeros((STRETCH, 128), F32) if i == 0 else ml[j, at, :]
        ml[j, at, :] = jnp.where(lane == i, top, jnp.where(lane == i + 4, total, stats))

    def attend_slots(a, b, i):
        def body(n, _):
            j = jnp.where(n == 0, a, b)
            for g in range(8):
                attend(j, g, i)
            return 0

        lax.fori_loop(0, 1 if a == b else 2, body, 0)

    for j in (1, 2, 3):
        for q in range(4):
            qup[j, q].wait_recv()
            qdown[8 - j, q].wait_recv()
            qsend(j, q)
            qsend(8 - j, q)
            if (j, q) == (1, 1):
                kvwait(0)
                attend_slots(0, 0, 0)
                kvsend(8)
            if (j, q) == (1, 3):
                osend(4)
                kvsend(10)
            if (j, q) == (2, 0):
                attend_slots(1, 7, 0)
            if (j, q) == (2, 2):
                kvwait(1)
                attend_slots(0, 0, 1)
            if (j, q) == (2, 3):
                attend_slots(1, 7, 1)
            if (j, q) == (3, 0):
                attend_slots(2, 6, 0)
            if (j, q) == (3, 1):
                kvsend(11)
                attend_slots(2, 6, 1)
    attend_slots(3, 5, 0)
    attend_slots(3, 5, 1)
    kvwait(2)
    attend_slots(0, 0, 2)
    attend_slots(1, 7, 2)
    attend_slots(2, 6, 2)
    attend_slots(3, 5, 2)
    oup[4].wait_recv()
    odown[4].wait_recv()

    own[2].wait()
    oxs = {}
    lower, upper = wog.at[pl.ds(0, 4), x], wog.at[pl.ds(4, 4), x]
    oxs["r"] = send(lower, lower, seq=right)
    oxs["l"] = send(upper, upper, seq=left)
    oxs["r1"] = send(upper, upper, seq=right)
    oxs["l1"] = send(lower, lower, seq=left)
    for q in range(4):
        (qup if q < 2 else qdown)[4, q].wait_recv()
    for i in range(3):
        attend_slots(4, 4, i)
    kvwait(3)
    attend_slots(4, 4, 3)

    sent, sent_stats = {}, {}

    def rsend(way, k, q, rows_at):
        j = k if way == 0 else 8 - k
        there = down if way == 0 else up
        sent[way, k, q] = send(oatt.at[j, rows_at], ro.at[way, k - 1, rows_at], seq=there)
        sent_stats[way, k, q] = send(sw.at[j, q], rw.at[way, k - 1, q], seq=there)

    def turn_out(j, q):
        sw[j, q] = jnp.transpose(ml[j, quarter(q), :])[0:8, :]

    def turn_in(way, k, q):
        wire = jnp.concatenate([rw[way, k - 1, q], jnp.zeros((120, 128), F32)], axis=0)
        return jnp.transpose(wire)

    def merge(way, k, q, start, size):
        j = k if way == 0 else 8 - k
        at = pl.ds(q * QT + start, size)
        a = turn_in(way, k + 1, q)[start : start + size]
        b = ml[j, at, :]
        top = jnp.maximum(a, b)
        ea, eb = jnp.exp(a - top), jnp.exp(b - top)
        total = a * pltpu.roll(ea, 4, axis=1) + b * pltpu.roll(eb, 4, axis=1)
        lanes = lax.broadcasted_iota(jnp.int32, (size, 128), 1)
        ml[j, at, :] = jnp.where(lanes < 4, top, jnp.where(lanes < 8, total, 0.0))
        for i in range(W // HD):
            cols = slice(i * HD, i * HD + HD)
            mixed = ea[:, i : i + 1] * ro[way, k, at, cols].astype(F32)
            mixed = mixed + eb[:, i : i + 1] * oatt[j, at, cols].astype(F32)
            oatt[j, at, cols] = mixed.astype(BF)

    def weights_for(g):
        return jnp.concatenate([wog[g, i] for i in range(NX)], axis=1)

    def join(q):
        at = quarter(q)
        for way in (0, 1):
            sent[way, 1, q].wait_recv()
            sent_stats[way, 1, q].wait_recv()
        a, b, e = turn_in(0, 1, q), turn_in(1, 1, q), ml[0, at, :]
        top = jnp.maximum(jnp.maximum(a, b), e)
        fa, fb, fe = jnp.exp(a - top), jnp.exp(b - top), jnp.exp(e - top)
        total = a * pltpu.roll(fa, 4, axis=1) + b * pltpu.roll(fb, 4, axis=1)
        total = total + e * pltpu.roll(fe, 4, axis=1)
        total = pltpu.roll(total, 124, axis=1)
        fa, fb, fe = fa / total, fb / total, fe / total
        for i in range(W // HD):
            cols = slice(i * HD, i * HD + HD)
            mixed = fa[:, i : i + 1] * ro[0, 0, at, cols].astype(F32)
            mixed = mixed + fb[:, i : i + 1] * ro[1, 0, at, cols].astype(F32)
            mixed = mixed + fe[:, i : i + 1] * oatt[0, at, cols].astype(F32)
            ctx[q, :, cols] = mixed.astype(BF)

    pairs, seconds, thirds, written = {}, {}, {}, []

    far_first = (2, 1, 3, 0)

    def for_twin(q):
        for i in far_first:
            g = 2 * ((y + i) % NY) + 1 - c
            ps[q, i] = jnp.dot(ctx[q], weights_for(g), preferred_element_type=F32).astype(BF)
            pairs[q, i] = send(ps.at[q, i], pr.at[q, i], head=twin)

    def for_self(q):
        for i in far_first:
            g = 2 * ((y + i) % NY) + c
            term = jnp.dot(ctx[q], weights_for(g), preferred_element_type=F32)
            pairs[q, i].wait_recv()
            term = term + pr[q, i].astype(F32)
            if i != 2:
                tf[q, i] = term
                continue
            t2s[q] = term.astype(BF)
            a, b = pl.ds(0, 64), pl.ds(64, 64)
            seconds[q] = (
                send(t2s.at[q, a], t2r.at[q, a], head=yup),
                send(t2s.at[q, b], t2r.at[q, b], head=ydown),
            )

    def pass_on(q):
        for copy in seconds[q]:
            copy.wait_recv()
        t1s[q, 0, 0:64] = (tf[q, 1, 0:64] + t2r[q, 0:64].astype(F32)).astype(BF)
        t1s[q, 0, 64:128] = tf[q, 1, 64:128].astype(BF)
        t1s[q, 1, 0:64] = tf[q, 3, 0:64].astype(BF)
        t1s[q, 1, 64:128] = (tf[q, 3, 64:128] + t2r[q, 64:128].astype(F32)).astype(BF)
        thirds[q] = (
            send(t1s.at[q, 0], t1r.at[q, 0], head=yup),
            send(t1s.at[q, 1], t1r.at[q, 1], head=ydown),
        )

    def finish(q):
        for copy in thirds[q]:
            copy.wait_recv()
        total = tf[q, 0] + t1r[q, 0].astype(F32) + t1r[q, 1].astype(F32)
        fin[pl.ds(64 + q * QT, QT), :] = total

    def give_edge():
        edge_s[...] = fin[pl.ds(T, 64), :].astype(BF)
        return send(edge_s, edge_r, seq=after)

    def take_edge(copy):
        copy.wait_recv()
        fin[pl.ds(0, 64), :] = jnp.where(s == 0, 0.0, edge_r[...].astype(F32))

    def write(i):
        ost[i] = fin[pl.ds(i * QT + 1, QT), :].astype(BF)
        copy = pltpu.make_async_copy(ost.at[i], out.at[quarter(i)], osem.at[i])
        copy.start()
        written.append(copy)

    def open_wave(q):
        turn_out(4, q)
        rsend(0, 4, q, pl.ds(q * QT, 64))
        rsend(1, 4, q, pl.ds(q * QT + 64, 64))

    def hop(k, q):
        for way in (0, 1):
            sent[way, k + 1, q].wait_recv()
            sent_stats[way, k + 1, q].wait_recv()
            if k == 3:
                merge(way, k, q, 64 * way, 64)
            else:
                merge(way, k, q, 0, QT)
            turn_out(k if way == 0 else 8 - k, q)
            rsend(way, k, q, quarter(q))

    first, second = (3, 0), (1, 2)
    for q in first:
        open_wave(q)
    attend_slots(3, 5, 3)
    for q in first:
        hop(3, q)
    for q in second:
        open_wave(q)
    attend_slots(2, 6, 3)
    for q in first:
        hop(2, q)
    attend_slots(1, 7, 3)
    attend_slots(0, 0, 3)
    for q in second:
        hop(3, q)
    oxs["r"].wait_recv()
    lower = wog.at[pl.ds(0, 4), lo]
    oxs["r2"] = send(lower, lower, seq=right)
    oxs["l"].wait_recv()
    upper = wog.at[pl.ds(4, 4), hi]
    oxs["l2"] = send(upper, upper, seq=left)
    for q in first:
        hop(1, q)
    for q in second:
        hop(2, q)
    for q in first:
        join(q)
    for name in ("r1", "l1", "r2", "l2"):
        oxs[name].wait_recv()
    for q in first:
        for_twin(q)
    for q in second:
        hop(1, q)
    for q in first:
        for_self(q)
    for q in first:
        pass_on(q)
    finish(3)
    edge = give_edge()
    finish(0)
    join(1)
    for_twin(1)
    join(2)
    for_twin(2)
    for_self(1)
    for_self(2)
    take_edge(edge)
    write(0)
    pass_on(1)
    pass_on(2)
    finish(1)
    write(1)
    finish(2)
    write(2)
    write(3)
    for copy in written:
        copy.wait()
    for copy in started.values():
        copy.wait_send()


def exchange(states, w_query, w_output, kv_store, ids, table):
    anywhere = pl.BlockSpec(memory_space=pl.ANY)
    vm = pltpu.VMEM
    return pl.pallas_call(
        kernel,
        out_shape=jax.ShapeDtypeStruct((T, W), BF),
        in_specs=[anywhere] * 5 + [pl.BlockSpec(memory_space=pltpu.SMEM)],
        out_specs=anywhere,
        scratch_shapes=[
            vm((T + 64, NHEAD * W), BF),
            vm((NZ, 512, W), BF),
            vm((T + 64, W), F32),
            vm((NZ, T, W), BF),
            *[vm((32, 2, NB_TOK, HD), BF)] * 4,
            vm((NZ, T, W), BF),
            vm((NZ, T, 128), F32),
            vm((2, 4, T, W), BF),
            vm((NZ, 4, 8, 128), F32),
            vm((2, 4, 4, 8, 128), F32),
            vm((NZ, NX, W, 128), BF),
            vm((NZ, 2, 8), jnp.int32),
            pltpu.SMEM((NZ, 2, 8), jnp.int32),
            vm((4, QT, W), BF),
            vm((4, NY, QT, 512), BF),
            vm((4, NY, QT, 512), BF),
            vm((4, NY, QT, 512), F32),
            vm((4, QT, 512), BF),
            vm((4, QT, 512), BF),
            vm((4, 2, QT, 512), BF),
            vm((4, 2, QT, 512), BF),
            vm((8, NB_TOK, W), BF),
            vm((T + 64, W), F32),
            vm((64, W), BF),
            vm((64, W), BF),
            vm((4, QT, 512), BF),
            pltpu.SemaphoreType.DMA((12,)),
            pltpu.SemaphoreType.DMA((4,)),
            pltpu.SemaphoreType.DMA((N_COPIES,)),
            pltpu.SemaphoreType.DMA((N_COPIES,)),
        ],
        compiler_params=pltpu.CompilerParams(
            collective_id=0, has_side_effects=True, vmem_limit_bytes=60 * 2**20
        ),
        cost_estimate=pl.CostEstimate(
            flops=8 * 10**9, bytes_accessed=8 * 2**20, transcendentals=2**22
        ),
    )(states, w_query, w_output, kv_store, ids, table)


def local(states, w_query, w_output, kv_store, neighbour_ids, block_row):
    return exchange(states, w_query, w_output, kv_store, neighbour_ids.T, block_row)


def solution(mesh):
    in_specs = (
        P("seq", None),
        P("seq", "head"),
        P("head", "seq"),
        P("seq", None, None, "head"),
        P("seq", None),
        P(),
    )
    out_specs = P("seq", "head")
    return jax.shard_map(local, mesh=mesh, in_specs=in_specs, out_specs=out_specs, check_vma=False)
```

```python
import jax
import jax.numpy as jnp
from jax import lax
from jax.experimental import pallas as pl
from jax.experimental.pallas import tpu as pltpu
from jax.sharding import PartitionSpec as P

HD = 128
STRETCH = 64
NB_TOK = 128
NX, NZ, NY = 4, 8, 4
NSEQ, NHEAD = NX * NZ, 2 * NY
T = 512
W = 512
QT = 128
NEG = -1e30
SCALE = 1.0 / HD**0.5
MESH = pl.DeviceIdType.MESH
N_COPIES = 232
PA, PB = 96, 32
AU, BU = (PA // 16 + 1) // 2 * 16, (PB // 16 + 1) // 2 * 16
BF = jnp.bfloat16
F32 = jnp.float32


def quarter(i):
    return pl.ds(i * QT, QT)


def part(i):
    return pl.ds(pl.multiple_of(i * QT, QT), QT)


def kernel(
    states, wq, wo, kv, ids, table, out,
    st, wqg, acc, qall, kv0, kv1, kv2, kv3, oatt, ml, ro, sw, rw, wog, iall, ism,
    ctx, ps, pr, tf, t2s, t2r, t1s, t1r, kraw, fin, edge_s, edge_r, ost, lsem, osem, ssem, rsem,
):
    s, h = lax.axis_index("seq"), lax.axis_index("head")
    z, x, y, c = s // NX, s % NX, h // 2, h % 2
    up, down = (s + NX) % NSEQ, (s + NSEQ - NX) % NSEQ
    right, left = z * NX + (x + 1) % NX, z * NX + (x + NX - 1) % NX
    after, before = (s + 1) % NSEQ, (s + NSEQ - 1) % NSEQ
    yup, ydown, twin = (h + 2) % NHEAD, (h + NHEAD - 2) % NHEAD, h + 1 - 2 * c
    kvh = (kv0, kv1, kv2, kv3)
    count = [0]
    started = {}

    def send(src, dst, seq=None, head=None):
        n = count[0]
        count[0] += 1
        copy = pltpu.make_async_remote_copy(
            src_ref=src,
            dst_ref=dst,
            send_sem=ssem.at[n],
            recv_sem=rsem.at[n],
            device_id=(s if seq is None else seq, h if head is None else head),
            device_id_type=MESH,
        )
        copy.start()
        started[id(copy)] = copy
        return copy

    barrier = pltpu.get_barrier_semaphore()
    peers = [((s + NX * i) % NSEQ, h) for i in range(1, NZ)]
    peers += [(right, h), (left, h), (after, h), (before, h)]
    peers += [(s, (h + i) % NHEAD) for i in range(1, NHEAD)]
    for peer in peers:
        pl.semaphore_signal(barrier, inc=1, device_id=peer, device_id_type=MESH)

    own = [
        pltpu.make_async_copy(states, st.at[pl.ds(0, T)], lsem.at[0]),
        pltpu.make_async_copy(wq, wqg.at[0, part(x)], lsem.at[1]),
        pltpu.make_async_copy(wo, wog.at[z, x], lsem.at[2]),
        pltpu.make_async_copy(ids, iall.at[0], lsem.at[3]),
        pltpu.make_async_copy(kv.at[:, 0], kraw, lsem.at[4]),
    ]
    own_values = [
        pltpu.make_async_copy(
            kv.at[:, 1, :, pl.ds(i * HD, HD)], kvh[i].at[pl.ds(x * 8, 8), 1], lsem.at[8 + i]
        )
        for i in range(4)
    ]
    own[4].start()
    for copy in own_values:
        copy.start()
    for i in (1, 0, 2, 3):
        own[i].start()

    pl.semaphore_wait(barrier, len(peers))

    def arows(d, start=0, size=PA):
        return pl.ds(pl.multiple_of(((x + NX - d) % NX) * QT + start, 16), size)

    def brows(xo, start=0, size=PB):
        return pl.ds(pl.multiple_of(xo * QT + PA + start, 16), size)

    wx, bup, bdown = {}, {}, {}
    wup, wdown = {}, {}

    def bsend(step):
        src = wq.at[pl.ds(PA, PB)]
        if step == 1:
            bup[1] = send(src, wqg.at[1, brows(x)], seq=up)
            bdown[1] = send(src, wqg.at[7, brows(x)], seq=down)
            return
        at = brows(x) if step < 4 else brows(x, 0, BU)
        bup[step - 1].wait_recv()
        bup[step] = send(wqg.at[step - 1, at], wqg.at[step, at], seq=up)
        at = brows(x) if step < 4 else brows(x, BU, PB - BU)
        bdown[step - 1].wait_recv()
        bdown[step] = send(wqg.at[9 - step, at], wqg.at[8 - step, at], seq=down)

    def wsend(j, d, first=False):
        at = arows(d)
        src = wq.at[pl.ds(0, PA)] if first else wqg.at[j, at]
        if j < 3 or (j == 3 and d in (0, 1)):
            wup[j + 1, d] = send(src, wqg.at[j + 1, at], seq=up)
        if j in (0, 7, 6) or (j == 5 and d in (2, 3)):
            wdown[(j + 7) % 8, d] = send(src, wqg.at[(j + 7) % 8, at], seq=down)

    wx[1] = send(wq.at[pl.ds(0, PA)], wqg.at[0, arows(0)], seq=right)
    wx[3] = send(wq.at[pl.ds(0, PA)], wqg.at[0, arows(0)], seq=left)
    bsend(1)
    wsend(0, 0, first=True)

    own[4].wait()

    def turn_keys(b, _):
        for i in range(W // HD):
            cols = slice(i * HD, i * HD + HD)
            kvh[i][x * 8 + b, 0] = jnp.transpose(kraw[b, :, cols])
        return 0

    lax.fori_loop(0, 8, turn_keys, 0)
    wx[1].wait_recv()
    wx[2] = send(wqg.at[0, arows(1, 0, AU)], wqg.at[0, arows(1, 0, AU)], seq=right)
    wx[3].wait_recv()
    wx[4] = send(wqg.at[0, arows(3, AU, PA - AU)], wqg.at[0, arows(3, AU, PA - AU)], seq=left)
    wsend(0, 1)
    wsend(0, 3)
    bsend(2)
    iids = [send(ids, iall.at[i], seq=(s + NX * i) % NSEQ) for i in range(1, NZ)]
    hcols = pl.ds(pl.multiple_of(h * W, W), W)
    tail = st.at[pl.ds(T, 64), hcols]
    first_rows = send(states.at[pl.ds(0, 64), hcols], tail, seq=before)

    lo, hi = (x + 3) % NX, (x + 1) % NX
    kvright, kvleft = {}, {}
    for copy in own_values:
        copy.wait()

    def blocks(i, xo, half):
        return kvh[i].at[pl.ds(xo * 8 + 4 * half, 4)]

    def kvsend(n):
        i, turn = n // 3, n % 3
        if turn < 2:
            a, b = blocks(i, x, turn), blocks(i, x, 1 - turn)
        else:
            a, b = blocks(i, lo, 0), blocks(i, hi, 1)
            kvright[3 * i].wait_recv()
            kvleft[3 * i].wait_recv()
        kvright[n] = send(a, a, seq=right)
        kvleft[n] = send(b, b, seq=left)

    def kvwait(i):
        for n in (3 * i + 1, 3 * i + 2):
            kvright[n].wait_recv()
            kvleft[n].wait_recv()

    def forward(j, d):
        wup[j, d].wait_recv()
        wdown[8 - j, d].wait_recv()
        wsend(j, d)
        wsend(8 - j, d)

    kvsend(0)
    wx[2].wait_recv()
    wx[4].wait_recv()
    wsend(0, 2)
    bsend(3)
    forward(1, 0)
    forward(1, 1)
    kvsend(1)
    bsend(4)
    forward(1, 3)
    first_rows.wait_recv()
    others = [send(tail, tail, head=(h + i) % NHEAD) for i in range(1, NHEAD)]
    own[1].wait()
    bup[4].wait_recv()
    bdown[4].wait_recv()
    bx = {}
    bx["r"] = send(wqg.at[:, brows(x)], wqg.at[:, brows(x)], seq=right)
    bx["l"] = send(wqg.at[:, brows(x)], wqg.at[:, brows(x)], seq=left)
    kvsend(2)
    forward(1, 2)

    oup, odown = {}, {}

    def osend(step):
        if step == 1:
            oup[1] = send(wo, wog.at[z, x], seq=up)
            odown[1] = send(wo, wog.at[z, x], seq=down)
            return
        oup[step - 1].wait_recv()
        a = (z + NZ - step + 1) % NZ
        if step < 4:
            oup[step] = send(wog.at[a, x], wog.at[a, x], seq=up)
        else:
            half = pl.ds(0, 256)
            oup[step] = send(wog.at[a, x, half], wog.at[a, x, half], seq=up)
        odown[step - 1].wait_recv()
        b = (z + step - 1) % NZ
        if step < 4:
            odown[step] = send(wog.at[b, x], wog.at[b, x], seq=down)
        else:
            half = pl.ds(256, 256)
            odown[step] = send(wog.at[b, x, half], wog.at[b, x, half], seq=down)

    def multiply(j):
        cols = pl.ds(pl.multiple_of(((z + NZ - j) % NZ) * 512, 512), 512)

        def body(i, _):
            r = pl.ds(pl.multiple_of(i * 192, 64), 192)
            term = jnp.dot(st[r, cols], wqg[j], preferred_element_type=F32)
            acc[r, :] = term if j == 0 else acc[r, :] + term
            return 0

        lax.fori_loop(0, 3, body, 0)

    osend(1)
    forward(2, 0)
    forward(2, 1)
    bx["r"].wait_recv()
    at = (pl.ds(0, 4), brows(lo))
    bx["r2"] = send(wqg.at[at], wqg.at[at], seq=right)
    bx["l"].wait_recv()
    at = (pl.ds(4, 4), brows(hi))
    bx["l2"] = send(wqg.at[at], wqg.at[at], seq=left)
    kvsend(3)
    forward(2, 3)
    forward(2, 2)
    osend(2)
    kvsend(4)
    kvsend(6)
    forward(3, 0)
    own[0].wait()
    for copy in others:
        copy.wait_recv()
    for copy in others:
        copy.wait_send()
        del started[id(copy)]
    forward(3, 1)

    @pl.when(s == NSEQ - 1)
    def _():
        st[pl.ds(T, 64), :] = jnp.zeros((64, NHEAD * W), BF)

    forward(3, 3)
    forward(3, 2)
    osend(3)
    kvsend(5)
    kvsend(7)
    bx["r2"].wait_recv()
    bx["l2"].wait_recv()
    for n in (0, 1, 7, 2, 6, 3, 5):
        multiply(n)
    for d in (0, 1):
        wup[4, d].wait_recv()
    for d in (2, 3):
        wdown[4, d].wait_recv()
    multiply(4)

    qup, qdown = {}, {}

    def qsend(j, q):
        at = qall.at[j, quarter(q)]
        if j < 3 or (j == 3 and q < 2):
            qup[j + 1, q] = send(at, qall.at[j + 1, quarter(q)], seq=up)
        if j in (0, 7, 6) or (j == 5 and q >= 2):
            k = (j + 7) % 8
            qdown[k, q] = send(at, qall.at[k, quarter(q)], seq=down)

    for q in range(4):
        qall[0, quarter(q), :] = acc[pl.ds(63 + q * QT, QT), :].astype(BF)
        qsend(0, q)

    kvsend(9)
    for copy in iids:
        copy.wait_recv()
    own[3].wait()
    scalars = pltpu.make_async_copy(iall, ism, lsem.at[5])
    scalars.start()
    scalars.wait()

    lane = lax.broadcasted_iota(jnp.int32, (STRETCH, 128), 1)
    wide = lax.broadcasted_iota(jnp.int32, (1, 2 * NB_TOK), 1)

    def attend(j, g, i):
        r0, r1 = table[ism[j, 0, g]], table[ism[j, 1, g]]
        off0 = jnp.where(r0 // 32 == z, 0.0, NEG)
        off1 = jnp.where(r1 // 32 == z, 0.0, NEG)
        bias = jnp.where(wide < NB_TOK, off0, off1)
        b0, b1 = r0 % 32, r1 % 32
        at = pl.ds(g * STRETCH, STRETCH)
        cols = slice(i * HD, i * HD + HD)
        keys = jnp.concatenate([kvh[i][b0, 0], kvh[i][b1, 0]], axis=1)
        scores = jnp.dot(qall[j, at, cols], keys, preferred_element_type=F32)
        scores = scores * SCALE + bias
        top = jnp.max(scores, axis=1, keepdims=True)
        weights = jnp.exp(scores - top).astype(BF)
        total = jnp.sum(weights.astype(F32), axis=1, keepdims=True)
        values = jnp.concatenate([kvh[i][b0, 1], kvh[i][b1, 1]], axis=0)
        got = jnp.dot(weights, values, preferred_element_type=F32)
        oatt[j, at, cols] = got.astype(BF)
        stats = jnp.zeros((STRETCH, 128), F32) if i == 0 else ml[j, at, :]
        ml[j, at, :] = jnp.where(lane == i, top, jnp.where(lane == i + 4, total, stats))

    def attend_slots(a, b, i):
        def body(n, _):
            j = jnp.where(n == 0, a, b)
            for g in range(8):
                attend(j, g, i)
            return 0

        lax.fori_loop(0, 1 if a == b else 2, body, 0)

    for j in (1, 2, 3):
        for q in range(4):
            qup[j, q].wait_recv()
            qdown[8 - j, q].wait_recv()
            qsend(j, q)
            qsend(8 - j, q)
            if (j, q) == (1, 1):
                kvwait(0)
                attend_slots(0, 0, 0)
                kvsend(8)
            if (j, q) == (1, 3):
                osend(4)
                kvsend(10)
            if (j, q) == (2, 0):
                attend_slots(1, 7, 0)
            if (j, q) == (2, 2):
                kvwait(1)
                attend_slots(0, 0, 1)
            if (j, q) == (2, 3):
                attend_slots(1, 7, 1)
            if (j, q) == (3, 0):
                attend_slots(2, 6, 0)
            if (j, q) == (3, 1):
                kvsend(11)
                attend_slots(2, 6, 1)
    attend_slots(3, 5, 0)
    attend_slots(3, 5, 1)
    kvwait(2)
    attend_slots(0, 0, 2)
    attend_slots(1, 7, 2)
    attend_slots(2, 6, 2)
    attend_slots(3, 5, 2)
    oup[4].wait_recv()
    odown[4].wait_recv()

    own[2].wait()
    oxs = {}
    lower, upper = wog.at[pl.ds(0, 4), x], wog.at[pl.ds(4, 4), x]
    oxs["r"] = send(lower, lower, seq=right)
    oxs["l"] = send(upper, upper, seq=left)
    oxs["r1"] = send(upper, upper, seq=right)
    oxs["l1"] = send(lower, lower, seq=left)
    for q in range(4):
        (qup if q < 2 else qdown)[4, q].wait_recv()
    for i in range(3):
        attend_slots(4, 4, i)
    kvwait(3)
    attend_slots(4, 4, 3)

    sent, sent_stats = {}, {}

    def rsend(way, k, q, rows_at):
        j = k if way == 0 else 8 - k
        there = down if way == 0 else up
        sent[way, k, q] = send(oatt.at[j, rows_at], ro.at[way, k - 1, rows_at], seq=there)
        sent_stats[way, k, q] = send(sw.at[j, q], rw.at[way, k - 1, q], seq=there)

    def turn_out(j, q):
        sw[j, q] = jnp.transpose(ml[j, quarter(q), :])[0:8, :]

    def turn_in(way, k, q):
        wire = jnp.concatenate([rw[way, k - 1, q], jnp.zeros((120, 128), F32)], axis=0)
        return jnp.transpose(wire)

    def merge(way, k, q, start, size):
        j = k if way == 0 else 8 - k
        at = pl.ds(q * QT + start, size)
        a = turn_in(way, k + 1, q)[start : start + size]
        b = ml[j, at, :]
        top = jnp.maximum(a, b)
        ea, eb = jnp.exp(a - top), jnp.exp(b - top)
        total = a * pltpu.roll(ea, 4, axis=1) + b * pltpu.roll(eb, 4, axis=1)
        lanes = lax.broadcasted_iota(jnp.int32, (size, 128), 1)
        ml[j, at, :] = jnp.where(lanes < 4, top, jnp.where(lanes < 8, total, 0.0))
        for i in range(W // HD):
            cols = slice(i * HD, i * HD + HD)
            mixed = ea[:, i : i + 1] * ro[way, k, at, cols].astype(F32)
            mixed = mixed + eb[:, i : i + 1] * oatt[j, at, cols].astype(F32)
            oatt[j, at, cols] = mixed.astype(BF)

    def weights_for(g):
        return jnp.concatenate([wog[g, i] for i in range(NX)], axis=1)

    def join(q):
        at = quarter(q)
        for way in (0, 1):
            sent[way, 1, q].wait_recv()
            sent_stats[way, 1, q].wait_recv()
        a, b, e = turn_in(0, 1, q), turn_in(1, 1, q), ml[0, at, :]
        top = jnp.maximum(jnp.maximum(a, b), e)
        fa, fb, fe = jnp.exp(a - top), jnp.exp(b - top), jnp.exp(e - top)
        total = a * pltpu.roll(fa, 4, axis=1) + b * pltpu.roll(fb, 4, axis=1)
        total = total + e * pltpu.roll(fe, 4, axis=1)
        total = pltpu.roll(total, 124, axis=1)
        fa, fb, fe = fa / total, fb / total, fe / total
        for i in range(W // HD):
            cols = slice(i * HD, i * HD + HD)
            mixed = fa[:, i : i + 1] * ro[0, 0, at, cols].astype(F32)
            mixed = mixed + fb[:, i : i + 1] * ro[1, 0, at, cols].astype(F32)
            mixed = mixed + fe[:, i : i + 1] * oatt[0, at, cols].astype(F32)
            ctx[q, :, cols] = mixed.astype(BF)

    pairs, seconds, thirds, written = {}, {}, {}, []

    far_first = (2, 1, 3, 0)

    def for_twin(q):
        for i in far_first:
            g = 2 * ((y + i) % NY) + 1 - c
            ps[q, i] = jnp.dot(ctx[q], weights_for(g), preferred_element_type=F32).astype(BF)
            pairs[q, i] = send(ps.at[q, i], pr.at[q, i], head=twin)

    def for_self(q):
        for i in far_first:
            g = 2 * ((y + i) % NY) + c
            term = jnp.dot(ctx[q], weights_for(g), preferred_element_type=F32)
            pairs[q, i].wait_recv()
            term = term + pr[q, i].astype(F32)
            if i != 2:
                tf[q, i] = term
                continue
            t2s[q] = term.astype(BF)
            a, b = pl.ds(0, 64), pl.ds(64, 64)
            seconds[q] = (
                send(t2s.at[q, a], t2r.at[q, a], head=yup),
                send(t2s.at[q, b], t2r.at[q, b], head=ydown),
            )

    def pass_on(q):
        for copy in seconds[q]:
            copy.wait_recv()
        t1s[q, 0, 0:64] = (tf[q, 1, 0:64] + t2r[q, 0:64].astype(F32)).astype(BF)
        t1s[q, 0, 64:128] = tf[q, 1, 64:128].astype(BF)
        t1s[q, 1, 0:64] = tf[q, 3, 0:64].astype(BF)
        t1s[q, 1, 64:128] = (tf[q, 3, 64:128] + t2r[q, 64:128].astype(F32)).astype(BF)
        thirds[q] = (
            send(t1s.at[q, 0], t1r.at[q, 0], head=yup),
            send(t1s.at[q, 1], t1r.at[q, 1], head=ydown),
        )

    def finish(q):
        for copy in thirds[q]:
            copy.wait_recv()
        total = tf[q, 0] + t1r[q, 0].astype(F32) + t1r[q, 1].astype(F32)
        fin[pl.ds(64 + q * QT, QT), :] = total

    def give_edge():
        edge_s[...] = fin[pl.ds(T, 64), :].astype(BF)
        return send(edge_s, edge_r, seq=after)

    def take_edge(copy):
        copy.wait_recv()
        fin[pl.ds(0, 64), :] = jnp.where(s == 0, 0.0, edge_r[...].astype(F32))

    def write(i):
        ost[i] = fin[pl.ds(i * QT + 1, QT), :].astype(BF)
        copy = pltpu.make_async_copy(ost.at[i], out.at[quarter(i)], osem.at[i])
        copy.start()
        written.append(copy)

    def open_wave(q):
        turn_out(4, q)
        rsend(0, 4, q, pl.ds(q * QT, 64))
        rsend(1, 4, q, pl.ds(q * QT + 64, 64))

    def hop(k, q):
        for way in (0, 1):
            sent[way, k + 1, q].wait_recv()
            sent_stats[way, k + 1, q].wait_recv()
            if k == 3:
                merge(way, k, q, 64 * way, 64)
            else:
                merge(way, k, q, 0, QT)
            turn_out(k if way == 0 else 8 - k, q)
            rsend(way, k, q, quarter(q))

    first, second = (3, 0), (1, 2)
    for q in first:
        open_wave(q)
    attend_slots(3, 5, 3)
    for q in first:
        hop(3, q)
    for q in second:
        open_wave(q)
    attend_slots(2, 6, 3)
    for q in first:
        hop(2, q)
    attend_slots(1, 7, 3)
    attend_slots(0, 0, 3)
    for q in second:
        hop(3, q)
    oxs["r"].wait_recv()
    lower = wog.at[pl.ds(0, 4), lo]
    oxs["r2"] = send(lower, lower, seq=right)
    oxs["l"].wait_recv()
    upper = wog.at[pl.ds(4, 4), hi]
    oxs["l2"] = send(upper, upper, seq=left)
    for q in first:
        hop(1, q)
    for q in second:
        hop(2, q)
    for q in first:
        join(q)
    for name in ("r1", "l1", "r2", "l2"):
        oxs[name].wait_recv()
    for q in first:
        for_twin(q)
    for q in second:
        hop(1, q)
    for q in first:
        for_self(q)
    for q in first:
        pass_on(q)
    join(1)
    for_twin(1)
    join(2)
    for_twin(2)
    for_self(1)
    for_self(2)
    finish(3)
    edge = give_edge()
    finish(0)
    pass_on(1)
    pass_on(2)
    take_edge(edge)
    write(0)
    finish(1)
    write(1)
    finish(2)
    write(2)
    write(3)
    for copy in written:
        copy.wait()
    for copy in started.values():
        copy.wait_send()


def exchange(states, w_query, w_output, kv_store, ids, table):
    anywhere = pl.BlockSpec(memory_space=pl.ANY)
    vm = pltpu.VMEM
    return pl.pallas_call(
        kernel,
        out_shape=jax.ShapeDtypeStruct((T, W), BF),
        in_specs=[anywhere] * 5 + [pl.BlockSpec(memory_space=pltpu.SMEM)],
        out_specs=anywhere,
        scratch_shapes=[
            vm((T + 64, NHEAD * W), BF),
            vm((NZ, 512, W), BF),
            vm((T + 64, W), F32),
            vm((NZ, T, W), BF),
            *[vm((32, 2, NB_TOK, HD), BF)] * 4,
            vm((NZ, T, W), BF),
            vm((NZ, T, 128), F32),
            vm((2, 4, T, W), BF),
            vm((NZ, 4, 8, 128), F32),
            vm((2, 4, 4, 8, 128), F32),
            vm((NZ, NX, W, 128), BF),
            vm((NZ, 2, 8), jnp.int32),
            pltpu.SMEM((NZ, 2, 8), jnp.int32),
            vm((4, QT, W), BF),
            vm((4, NY, QT, 512), BF),
            vm((4, NY, QT, 512), BF),
            vm((4, NY, QT, 512), F32),
            vm((4, QT, 512), BF),
            vm((4, QT, 512), BF),
            vm((4, 2, QT, 512), BF),
            vm((4, 2, QT, 512), BF),
            vm((8, NB_TOK, W), BF),
            vm((T + 64, W), F32),
            vm((64, W), BF),
            vm((64, W), BF),
            vm((4, QT, 512), BF),
            pltpu.SemaphoreType.DMA((12,)),
            pltpu.SemaphoreType.DMA((4,)),
            pltpu.SemaphoreType.DMA((N_COPIES,)),
            pltpu.SemaphoreType.DMA((N_COPIES,)),
        ],
        compiler_params=pltpu.CompilerParams(
            collective_id=0, has_side_effects=True, vmem_limit_bytes=60 * 2**20
        ),
        cost_estimate=pl.CostEstimate(
            flops=8 * 10**9, bytes_accessed=8 * 2**20, transcendentals=2**22
        ),
    )(states, w_query, w_output, kv_store, ids, table)


def local(states, w_query, w_output, kv_store, neighbour_ids, block_row):
    return exchange(states, w_query, w_output, kv_store, neighbour_ids.T, block_row)


def solution(mesh):
    in_specs = (
        P("seq", None),
        P("seq", "head"),
        P("head", "seq"),
        P("seq", None, None, "head"),
        P("seq", None),
        P(),
    )
    out_specs = P("seq", "head")
    return jax.shard_map(local, mesh=mesh, in_specs=in_specs, out_specs=out_specs, check_vma=False)
```

```python
import jax
import jax.numpy as jnp
from jax import lax
from jax.experimental import pallas as pl
from jax.experimental.pallas import tpu as pltpu
from jax.sharding import PartitionSpec as P

HD = 128
STRETCH = 64
NB_TOK = 128
NX, NZ, NY = 4, 8, 4
NSEQ, NHEAD = NX * NZ, 2 * NY
T = 512
W = 512
QT = 128
NEG = -1e30
SCALE = 1.0 / HD**0.5
MESH = pl.DeviceIdType.MESH
N_COPIES = 232
PA, PB = 96, 32
AU, BU = (PA // 16 + 1) // 2 * 16, (PB // 16 + 1) // 2 * 16
BF = jnp.bfloat16
F32 = jnp.float32


def quarter(i):
    return pl.ds(i * QT, QT)


def part(i):
    return pl.ds(pl.multiple_of(i * QT, QT), QT)


def kernel(
    states, wq, wo, kv, ids, table, out,
    st, wqg, acc, qall, kv0, kv1, kv2, kv3, oatt, ml, ro, sw, rw, wog, iall, ism,
    ctx, ps, pr, tf, t2s, t2r, t1s, t1r, kraw, fin, edge_s, edge_r, lsem, ssem, rsem,
):
    s, h = lax.axis_index("seq"), lax.axis_index("head")
    z, x, y, c = s // NX, s % NX, h // 2, h % 2
    up, down = (s + NX) % NSEQ, (s + NSEQ - NX) % NSEQ
    right, left = z * NX + (x + 1) % NX, z * NX + (x + NX - 1) % NX
    after, before = (s + 1) % NSEQ, (s + NSEQ - 1) % NSEQ
    yup, ydown, twin = (h + 2) % NHEAD, (h + NHEAD - 2) % NHEAD, h + 1 - 2 * c
    kvh = (kv0, kv1, kv2, kv3)
    count = [0]
    started = {}

    def send(src, dst, seq=None, head=None):
        n = count[0]
        count[0] += 1
        copy = pltpu.make_async_remote_copy(
            src_ref=src,
            dst_ref=dst,
            send_sem=ssem.at[n],
            recv_sem=rsem.at[n],
            device_id=(s if seq is None else seq, h if head is None else head),
            device_id_type=MESH,
        )
        copy.start()
        started[id(copy)] = copy
        return copy

    barrier = pltpu.get_barrier_semaphore()
    peers = [((s + NX * i) % NSEQ, h) for i in range(1, NZ)]
    peers += [(right, h), (left, h), (after, h), (before, h)]
    peers += [(s, (h + i) % NHEAD) for i in range(1, NHEAD)]
    for peer in peers:
        pl.semaphore_signal(barrier, inc=1, device_id=peer, device_id_type=MESH)

    own = [
        pltpu.make_async_copy(states, st.at[pl.ds(0, T)], lsem.at[0]),
        pltpu.make_async_copy(wq, wqg.at[0, part(x)], lsem.at[1]),
        pltpu.make_async_copy(wo, wog.at[z, x], lsem.at[2]),
        pltpu.make_async_copy(ids, iall.at[0], lsem.at[3]),
        pltpu.make_async_copy(kv.at[:, 0], kraw, lsem.at[4]),
    ]
    own_values = [
        pltpu.make_async_copy(
            kv.at[:, 1, :, pl.ds(i * HD, HD)], kvh[i].at[pl.ds(x * 8, 8), 1], lsem.at[8 + i]
        )
        for i in range(4)
    ]
    own[4].start()
    for copy in own_values:
        copy.start()
    for i in (1, 0, 2, 3):
        own[i].start()

    pl.semaphore_wait(barrier, len(peers))

    def arows(d, start=0, size=PA):
        return pl.ds(pl.multiple_of(((x + NX - d) % NX) * QT + start, 16), size)

    def brows(xo, start=0, size=PB):
        return pl.ds(pl.multiple_of(xo * QT + PA + start, 16), size)

    wx, bup, bdown = {}, {}, {}
    wup, wdown = {}, {}

    def bsend(step):
        src = wq.at[pl.ds(PA, PB)]
        if step == 1:
            bup[1] = send(src, wqg.at[1, brows(x)], seq=up)
            bdown[1] = send(src, wqg.at[7, brows(x)], seq=down)
            return
        at = brows(x) if step < 4 else brows(x, 0, BU)
        bup[step - 1].wait_recv()
        bup[step] = send(wqg.at[step - 1, at], wqg.at[step, at], seq=up)
        at = brows(x) if step < 4 else brows(x, BU, PB - BU)
        bdown[step - 1].wait_recv()
        bdown[step] = send(wqg.at[9 - step, at], wqg.at[8 - step, at], seq=down)

    def wsend(j, d, first=False):
        at = arows(d)
        src = wq.at[pl.ds(0, PA)] if first else wqg.at[j, at]
        if j < 3 or (j == 3 and d in (0, 1)):
            wup[j + 1, d] = send(src, wqg.at[j + 1, at], seq=up)
        if j in (0, 7, 6) or (j == 5 and d in (2, 3)):
            wdown[(j + 7) % 8, d] = send(src, wqg.at[(j + 7) % 8, at], seq=down)

    wx[1] = send(wq.at[pl.ds(0, PA)], wqg.at[0, arows(0)], seq=right)
    wx[3] = send(wq.at[pl.ds(0, PA)], wqg.at[0, arows(0)], seq=left)
    bsend(1)
    wsend(0, 0, first=True)

    own[4].wait()

    def turn_keys(b, _):
        for i in range(W // HD):
            cols = slice(i * HD, i * HD + HD)
            kvh[i][x * 8 + b, 0] = jnp.transpose(kraw[b, :, cols])
        return 0

    lax.fori_loop(0, 8, turn_keys, 0)
    wx[1].wait_recv()
    wx[2] = send(wqg.at[0, arows(1, 0, AU)], wqg.at[0, arows(1, 0, AU)], seq=right)
    wx[3].wait_recv()
    wx[4] = send(wqg.at[0, arows(3, AU, PA - AU)], wqg.at[0, arows(3, AU, PA - AU)], seq=left)
    wsend(0, 1)
    wsend(0, 3)
    bsend(2)
    iids = [send(ids, iall.at[i], seq=(s + NX * i) % NSEQ) for i in range(1, NZ)]
    hcols = pl.ds(pl.multiple_of(h * W, W), W)
    tail = st.at[pl.ds(T, 64), hcols]
    first_rows = send(states.at[pl.ds(0, 64), hcols], tail, seq=before)

    lo, hi = (x + 3) % NX, (x + 1) % NX
    kvright, kvleft = {}, {}
    for copy in own_values:
        copy.wait()

    def blocks(i, xo, half):
        return kvh[i].at[pl.ds(xo * 8 + 4 * half, 4)]

    def kvsend(n):
        i, turn = n // 3, n % 3
        if turn < 2:
            a, b = blocks(i, x, turn), blocks(i, x, 1 - turn)
        else:
            a, b = blocks(i, lo, 0), blocks(i, hi, 1)
            kvright[3 * i].wait_recv()
            kvleft[3 * i].wait_recv()
        kvright[n] = send(a, a, seq=right)
        kvleft[n] = send(b, b, seq=left)

    def kvwait(i):
        for n in (3 * i + 1, 3 * i + 2):
            kvright[n].wait_recv()
            kvleft[n].wait_recv()

    def forward(j, d):
        wup[j, d].wait_recv()
        wdown[8 - j, d].wait_recv()
        wsend(j, d)
        wsend(8 - j, d)

    kvsend(0)
    wx[2].wait_recv()
    wx[4].wait_recv()
    wsend(0, 2)
    bsend(3)
    forward(1, 0)
    forward(1, 1)
    kvsend(1)
    bsend(4)
    forward(1, 3)
    first_rows.wait_recv()
    others = [send(tail, tail, head=(h + i) % NHEAD) for i in range(1, NHEAD)]
    own[1].wait()
    bup[4].wait_recv()
    bdown[4].wait_recv()
    bx = {}
    bx["r"] = send(wqg.at[:, brows(x)], wqg.at[:, brows(x)], seq=right)
    bx["l"] = send(wqg.at[:, brows(x)], wqg.at[:, brows(x)], seq=left)
    kvsend(2)
    forward(1, 2)

    oup, odown = {}, {}

    def osend(step):
        if step == 1:
            oup[1] = send(wo, wog.at[z, x], seq=up)
            odown[1] = send(wo, wog.at[z, x], seq=down)
            return
        oup[step - 1].wait_recv()
        a = (z + NZ - step + 1) % NZ
        if step < 4:
            oup[step] = send(wog.at[a, x], wog.at[a, x], seq=up)
        else:
            half = pl.ds(0, 256)
            oup[step] = send(wog.at[a, x, half], wog.at[a, x, half], seq=up)
        odown[step - 1].wait_recv()
        b = (z + step - 1) % NZ
        if step < 4:
            odown[step] = send(wog.at[b, x], wog.at[b, x], seq=down)
        else:
            half = pl.ds(256, 256)
            odown[step] = send(wog.at[b, x, half], wog.at[b, x, half], seq=down)

    def multiply(j):
        cols = pl.ds(pl.multiple_of(((z + NZ - j) % NZ) * 512, 512), 512)

        def body(i, _):
            r = pl.ds(pl.multiple_of(i * 192, 64), 192)
            term = jnp.dot(st[r, cols], wqg[j], preferred_element_type=F32)
            acc[r, :] = term if j == 0 else acc[r, :] + term
            return 0

        lax.fori_loop(0, 3, body, 0)

    osend(1)
    forward(2, 0)
    forward(2, 1)
    bx["r"].wait_recv()
    at = (pl.ds(0, 4), brows(lo))
    bx["r2"] = send(wqg.at[at], wqg.at[at], seq=right)
    bx["l"].wait_recv()
    at = (pl.ds(4, 4), brows(hi))
    bx["l2"] = send(wqg.at[at], wqg.at[at], seq=left)
    kvsend(3)
    forward(2, 3)
    forward(2, 2)
    osend(2)
    kvsend(4)
    kvsend(6)
    forward(3, 0)
    own[0].wait()
    for copy in others:
        copy.wait_recv()
    for copy in others:
        copy.wait_send()
        del started[id(copy)]
    forward(3, 1)

    @pl.when(s == NSEQ - 1)
    def _():
        st[pl.ds(T, 64), :] = jnp.zeros((64, NHEAD * W), BF)

    forward(3, 3)
    forward(3, 2)
    osend(3)
    kvsend(5)
    kvsend(7)
    bx["r2"].wait_recv()
    bx["l2"].wait_recv()
    for n in (0, 1, 7, 2, 6, 3, 5):
        multiply(n)
    for d in (0, 1):
        wup[4, d].wait_recv()
    for d in (2, 3):
        wdown[4, d].wait_recv()
    multiply(4)

    qup, qdown = {}, {}

    def qsend(j, q):
        at = qall.at[j, quarter(q)]
        if j < 3 or (j == 3 and q < 2):
            qup[j + 1, q] = send(at, qall.at[j + 1, quarter(q)], seq=up)
        if j in (0, 7, 6) or (j == 5 and q >= 2):
            k = (j + 7) % 8
            qdown[k, q] = send(at, qall.at[k, quarter(q)], seq=down)

    for q in range(4):
        qall[0, quarter(q), :] = acc[pl.ds(63 + q * QT, QT), :].astype(BF)
        if q < 2:
            qsend(0, q)

    kvsend(9)
    for copy in iids:
        copy.wait_recv()
    own[3].wait()
    scalars = pltpu.make_async_copy(iall, ism, lsem.at[5])
    scalars.start()
    scalars.wait()
    for q in (2, 3):
        for copy in (qup[1, q - 2], qdown[7, q - 2]):
            copy.wait_send()
            del started[id(copy)]
        qsend(0, q)

    lane = lax.broadcasted_iota(jnp.int32, (STRETCH, 128), 1)
    wide = lax.broadcasted_iota(jnp.int32, (1, 2 * NB_TOK), 1)

    def attend(j, g, i):
        r0, r1 = table[ism[j, 0, g]], table[ism[j, 1, g]]
        off0 = jnp.where(r0 // 32 == z, 0.0, NEG)
        off1 = jnp.where(r1 // 32 == z, 0.0, NEG)
        bias = jnp.where(wide < NB_TOK, off0, off1)
        b0, b1 = r0 % 32, r1 % 32
        at = pl.ds(g * STRETCH, STRETCH)
        cols = slice(i * HD, i * HD + HD)
        keys = jnp.concatenate([kvh[i][b0, 0], kvh[i][b1, 0]], axis=1)
        scores = jnp.dot(qall[j, at, cols], keys, preferred_element_type=F32)
        scores = scores * SCALE + bias
        top = jnp.max(scores, axis=1, keepdims=True)
        weights = jnp.exp(scores - top).astype(BF)
        total = jnp.sum(weights.astype(F32), axis=1, keepdims=True)
        values = jnp.concatenate([kvh[i][b0, 1], kvh[i][b1, 1]], axis=0)
        got = jnp.dot(weights, values, preferred_element_type=F32)
        oatt[j, at, cols] = got.astype(BF)
        stats = jnp.zeros((STRETCH, 128), F32) if i == 0 else ml[j, at, :]
        ml[j, at, :] = jnp.where(lane == i, top, jnp.where(lane == i + 4, total, stats))

    def attend_slots(a, b, i):
        def body(n, _):
            j = jnp.where(n == 0, a, b)
            for g in range(8):
                attend(j, g, i)
            return 0

        lax.fori_loop(0, 1 if a == b else 2, body, 0)

    for j in (1, 2, 3):
        for q in range(4):
            qup[j, q].wait_recv()
            qdown[8 - j, q].wait_recv()
            qsend(j, q)
            qsend(8 - j, q)
            if (j, q) == (1, 1):
                kvwait(0)
                attend_slots(0, 0, 0)
                kvsend(8)
            if (j, q) == (1, 3):
                osend(4)
                kvsend(10)
            if (j, q) == (2, 0):
                attend_slots(1, 7, 0)
            if (j, q) == (2, 2):
                kvwait(1)
                attend_slots(0, 0, 1)
            if (j, q) == (2, 3):
                attend_slots(1, 7, 1)
            if (j, q) == (3, 0):
                attend_slots(2, 6, 0)
            if (j, q) == (3, 1):
                kvsend(11)
                attend_slots(2, 6, 1)
    attend_slots(3, 5, 0)
    attend_slots(3, 5, 1)
    kvwait(2)
    attend_slots(0, 0, 2)
    attend_slots(1, 7, 2)
    attend_slots(2, 6, 2)
    attend_slots(3, 5, 2)
    oup[4].wait_recv()
    odown[4].wait_recv()

    own[2].wait()
    oxs = {}
    lower, upper = wog.at[pl.ds(0, 4), x], wog.at[pl.ds(4, 4), x]
    oxs["r"] = send(lower, lower, seq=right)
    oxs["l"] = send(upper, upper, seq=left)
    oxs["r1"] = send(upper, upper, seq=right)
    oxs["l1"] = send(lower, lower, seq=left)
    for q in range(4):
        (qup if q < 2 else qdown)[4, q].wait_recv()
    for i in range(3):
        attend_slots(4, 4, i)
    kvwait(3)
    attend_slots(4, 4, 3)

    sent, sent_stats = {}, {}

    def rsend(way, k, q, rows_at):
        j = k if way == 0 else 8 - k
        there = down if way == 0 else up
        sent[way, k, q] = send(oatt.at[j, rows_at], ro.at[way, k - 1, rows_at], seq=there)
        sent_stats[way, k, q] = send(sw.at[j, q], rw.at[way, k - 1, q], seq=there)

    def turn_out(j, q):
        sw[j, q] = jnp.transpose(ml[j, quarter(q), :])[0:8, :]

    def turn_in(way, k, q):
        wire = jnp.concatenate([rw[way, k - 1, q], jnp.zeros((120, 128), F32)], axis=0)
        return jnp.transpose(wire)

    def merge(way, k, q, start, size):
        j = k if way == 0 else 8 - k
        at = pl.ds(q * QT + start, size)
        a = turn_in(way, k + 1, q)[start : start + size]
        b = ml[j, at, :]
        top = jnp.maximum(a, b)
        ea, eb = jnp.exp(a - top), jnp.exp(b - top)
        total = a * pltpu.roll(ea, 4, axis=1) + b * pltpu.roll(eb, 4, axis=1)
        lanes = lax.broadcasted_iota(jnp.int32, (size, 128), 1)
        ml[j, at, :] = jnp.where(lanes < 4, top, jnp.where(lanes < 8, total, 0.0))
        for i in range(W // HD):
            cols = slice(i * HD, i * HD + HD)
            mixed = ea[:, i : i + 1] * ro[way, k, at, cols].astype(F32)
            mixed = mixed + eb[:, i : i + 1] * oatt[j, at, cols].astype(F32)
            oatt[j, at, cols] = mixed.astype(BF)

    def weights_for(g):
        return jnp.concatenate([wog[g, i] for i in range(NX)], axis=1)

    def join(q):
        at = quarter(q)
        for way in (0, 1):
            sent[way, 1, q].wait_recv()
            sent_stats[way, 1, q].wait_recv()
        a, b, e = turn_in(0, 1, q), turn_in(1, 1, q), ml[0, at, :]
        top = jnp.maximum(jnp.maximum(a, b), e)
        fa, fb, fe = jnp.exp(a - top), jnp.exp(b - top), jnp.exp(e - top)
        total = a * pltpu.roll(fa, 4, axis=1) + b * pltpu.roll(fb, 4, axis=1)
        total = total + e * pltpu.roll(fe, 4, axis=1)
        total = pltpu.roll(total, 124, axis=1)
        fa, fb, fe = fa / total, fb / total, fe / total
        for i in range(W // HD):
            cols = slice(i * HD, i * HD + HD)
            mixed = fa[:, i : i + 1] * ro[0, 0, at, cols].astype(F32)
            mixed = mixed + fb[:, i : i + 1] * ro[1, 0, at, cols].astype(F32)
            mixed = mixed + fe[:, i : i + 1] * oatt[0, at, cols].astype(F32)
            ctx[q, :, cols] = mixed.astype(BF)

    pairs, seconds, thirds = {}, {}, {}

    far_first = (2, 1, 3, 0)

    def for_twin(q):
        for i in far_first:
            g = 2 * ((y + i) % NY) + 1 - c
            ps[q, i] = jnp.dot(ctx[q], weights_for(g), preferred_element_type=F32).astype(BF)
            pairs[q, i] = send(ps.at[q, i], pr.at[q, i], head=twin)

    def for_self(q):
        for i in far_first:
            g = 2 * ((y + i) % NY) + c
            term = jnp.dot(ctx[q], weights_for(g), preferred_element_type=F32)
            pairs[q, i].wait_recv()
            term = term + pr[q, i].astype(F32)
            if i != 2:
                tf[q, i] = term
                continue
            t2s[q] = term.astype(BF)
            a, b = pl.ds(0, 64), pl.ds(64, 64)
            seconds[q] = (
                send(t2s.at[q, a], t2r.at[q, a], head=yup),
                send(t2s.at[q, b], t2r.at[q, b], head=ydown),
            )

    def pass_on(q):
        for copy in seconds[q]:
            copy.wait_recv()
        t1s[q, 0, 0:64] = (tf[q, 1, 0:64] + t2r[q, 0:64].astype(F32)).astype(BF)
        t1s[q, 0, 64:128] = tf[q, 1, 64:128].astype(BF)
        t1s[q, 1, 0:64] = tf[q, 3, 0:64].astype(BF)
        t1s[q, 1, 64:128] = (tf[q, 3, 64:128] + t2r[q, 64:128].astype(F32)).astype(BF)
        thirds[q] = (
            send(t1s.at[q, 0], t1r.at[q, 0], head=yup),
            send(t1s.at[q, 1], t1r.at[q, 1], head=ydown),
        )

    def finish(q):
        for copy in thirds[q]:
            copy.wait_recv()
        total = tf[q, 0] + t1r[q, 0].astype(F32) + t1r[q, 1].astype(F32)
        fin[pl.ds(64 + q * QT, QT), :] = total

    def give_edge():
        edge_s[...] = fin[pl.ds(T, 64), :].astype(BF)
        return send(edge_s, edge_r, seq=after)

    def take_edge(copy):
        copy.wait_recv()
        fin[pl.ds(0, 64), :] = jnp.where(s == 0, 0.0, edge_r[...].astype(F32))

    def write(i):
        out[quarter(i), :] = fin[pl.ds(i * QT + 1, QT), :].astype(BF)

    def open_wave(q):
        turn_out(4, q)
        rsend(0, 4, q, pl.ds(q * QT, 64))
        rsend(1, 4, q, pl.ds(q * QT + 64, 64))

    def hop(k, q):
        for way in (0, 1):
            sent[way, k + 1, q].wait_recv()
            sent_stats[way, k + 1, q].wait_recv()
            if k == 3:
                merge(way, k, q, 64 * way, 64)
            else:
                merge(way, k, q, 0, QT)
            turn_out(k if way == 0 else 8 - k, q)
            rsend(way, k, q, quarter(q))

    first, second = (3, 0), (1, 2)
    for q in first:
        open_wave(q)
    attend_slots(3, 5, 3)
    for q in first:
        hop(3, q)
    for q in second:
        open_wave(q)
    attend_slots(2, 6, 3)
    for q in first:
        hop(2, q)
    attend_slots(1, 7, 3)
    attend_slots(0, 0, 3)
    for q in second:
        hop(3, q)
    oxs["r"].wait_recv()
    lower = wog.at[pl.ds(0, 4), lo]
    oxs["r2"] = send(lower, lower, seq=right)
    oxs["l"].wait_recv()
    upper = wog.at[pl.ds(4, 4), hi]
    oxs["l2"] = send(upper, upper, seq=left)
    for q in first:
        hop(1, q)
    for q in second:
        hop(2, q)
    for q in first:
        join(q)
    for name in ("r1", "l1", "r2", "l2"):
        oxs[name].wait_recv()
    for q in first:
        for_twin(q)
    for q in second:
        hop(1, q)
    for q in first:
        for_self(q)
    for q in first:
        pass_on(q)
    join(1)
    for_twin(1)
    join(2)
    for_twin(2)
    for_self(1)
    for_self(2)
    finish(3)
    edge = give_edge()
    finish(0)
    pass_on(1)
    pass_on(2)
    take_edge(edge)
    write(0)
    finish(1)
    write(1)
    finish(2)
    write(2)
    write(3)
    for copy in started.values():
        copy.wait_send()


def exchange(states, w_query, w_output, kv_store, ids, table):
    anywhere = pl.BlockSpec(memory_space=pl.ANY)
    vm = pltpu.VMEM
    return pl.pallas_call(
        kernel,
        out_shape=jax.ShapeDtypeStruct((T, W), BF),
        in_specs=[anywhere] * 5 + [pl.BlockSpec(memory_space=pltpu.SMEM)],
        out_specs=pl.BlockSpec(memory_space=vm),
        scratch_shapes=[
            vm((T + 64, NHEAD * W), BF),
            vm((NZ, 512, W), BF),
            vm((T + 64, W), F32),
            vm((NZ, T, W), BF),
            *[vm((32, 2, NB_TOK, HD), BF)] * 4,
            vm((NZ, T, W), BF),
            vm((NZ, T, 128), F32),
            vm((2, 4, T, W), BF),
            vm((NZ, 4, 8, 128), F32),
            vm((2, 4, 4, 8, 128), F32),
            vm((NZ, NX, W, 128), BF),
            vm((NZ, 2, 8), jnp.int32),
            pltpu.SMEM((NZ, 2, 8), jnp.int32),
            vm((4, QT, W), BF),
            vm((4, NY, QT, 512), BF),
            vm((4, NY, QT, 512), BF),
            vm((4, NY, QT, 512), F32),
            vm((4, QT, 512), BF),
            vm((4, QT, 512), BF),
            vm((4, 2, QT, 512), BF),
            vm((4, 2, QT, 512), BF),
            vm((8, NB_TOK, W), BF),
            vm((T + 64, W), F32),
            vm((64, W), BF),
            vm((64, W), BF),
            pltpu.SemaphoreType.DMA((12,)),
            pltpu.SemaphoreType.DMA((N_COPIES,)),
            pltpu.SemaphoreType.DMA((N_COPIES,)),
        ],
        compiler_params=pltpu.CompilerParams(
            collective_id=0, has_side_effects=True, vmem_limit_bytes=60 * 2**20
        ),
        cost_estimate=pl.CostEstimate(
            flops=8 * 10**9, bytes_accessed=8 * 2**20, transcendentals=2**22
        ),
    )(states, w_query, w_output, kv_store, ids, table)


def local(states, w_query, w_output, kv_store, neighbour_ids, block_row):
    return exchange(states, w_query, w_output, kv_store, neighbour_ids.T, block_row)


def solution(mesh):
    in_specs = (
        P("seq", None),
        P("seq", "head"),
        P("head", "seq"),
        P("seq", None, None, "head"),
        P("seq", None),
        P(),
    )
    out_specs = P("seq", "head")
    return jax.shard_map(local, mesh=mesh, in_specs=in_specs, out_specs=out_specs, check_vma=False)
```
